32 devices in a mesh: pix: 8 (over z, y), batch: 4 (over x, core).
Axes of the slice: x: 2, y: 2, z: 4, core: 2. Of those that a mesh axis runs over, the one named last changes fastest.
Arguments:
- fine_tokens: bfloat16 [32768, 512], P(('batch', 'pix')), parts along dimension 0, may hold values from -8 to 8
- parent_tokens: bfloat16 [8192, 512], P(('batch', 'pix')), parts along dimension 0, may hold values from -8 to 8
- shift_table: int32 [8192], P('pix'), may hold values from 0 to 8191, as said below
- parent_slot: int32 [2048], P('pix'), may hold values from 0 to 255, as said below
- fine_gain: float32 [512], replicated, may hold values from 0.1 to 1.9
- parent_gain: float32 [512], replicated, may hold values from 0.1 to 1.9
- w_qkv: bfloat16 [512, 1536], replicated, may hold values from -2 to 2
- w_parent: bfloat16 [512, 1024], replicated, may hold values from -2 to 2
- w_out: bfloat16 [1024, 512], replicated, may hold values from -0.1875 to 0.1875
Outputs:
- mixed: bfloat16 [32768, 512], P(('batch', 'pix')), parts along dimension 0
The draws below stay inside these ranges and needn't reach their ends.
There are 4 independent parts, one for each index of `batch`. The reference program is written for one: setup_inputs(seed, part) draws one part's arguments, and reference() takes and returns one part's arrays. A program takes and returns all parts, laid end to end along the dimension named above; an argument that names none is the same for every part. Nothing has to cross between parts.
Inputs may be any that keep to these rules, and one draw needn't show every extreme that they name: Every entry shift_table[p] equals (p + o) mod 8192 with -128 <= o <= 128; on every device one entry has o = 128 and one o = -128. Over the stored rows of one owner j, parent_slot takes every value 0 to 255 once.
All inputs are finite; a program needn't handle non-finite values.
Results may differ from the reference program's by a relative error of at most 0.0018.
The reference program's roundings to bfloat16 on the way count: a program that leaves them out, or rounds other values in their place, can miss the bound.
Values may be sent and summed in bfloat16 or wider, within the bound.
No kernel may reach another device: no remote copies, remote signals or barrier semaphores. Data moves between devices by JAX's collectives and lax.ppermute only.
A program may use at most 64 MiB of HBM per device.

```python
import jax
import jax.numpy as jnp
from jax import lax

D = 512
HEADS = 16
HD = 32
WIN = 256
HALO = 128
PWIN = 64
PIX_DEV = 1024
PAR_DEV = 256
NPIX = 8192
NPAR = 2048
N_PIX = 8


def draw_shift_table(key, part):
    everything = jnp.arange(NPIX, dtype=jnp.int32)
    offsets = jax.random.randint(key, (NPIX,), -HALO, HALO + 1, dtype=jnp.int32)
    within = everything % PIX_DEV
    offsets = jnp.where(within == 0, HALO, offsets)
    offsets = jnp.where(within == 1, -HALO, offsets)
    offsets = jnp.where(within == 2, -3, offsets)
    offsets = jnp.where(within == 3, -3, offsets)
    return jnp.mod(everything + offsets, NPIX).astype(jnp.int32)


def draw_parent_slot(key, part):
    owners = NPAR // PAR_DEV
    block_rows = PAR_DEV // owners
    subkeys = jax.random.split(jax.random.fold_in(key, 7), owners)
    orders = jax.vmap(lambda single: jax.random.permutation(single, PAR_DEV))(subkeys)
    table = orders.reshape(owners, owners, block_rows)
    return jnp.transpose(table, (1, 0, 2)).reshape(NPAR).astype(jnp.int32)


def draw_fine_tokens(key, part):
    sub = jax.random.fold_in(key, 31)
    values = jnp.clip(jax.random.normal(sub, (NPIX, D), jnp.float32), -6.0, 6.0)
    return values.astype(jnp.bfloat16)


def draw_parent_tokens(key, part):
    sub = jax.random.fold_in(key, 32)
    values = jnp.clip(jax.random.normal(sub, (NPAR, D), jnp.float32), -6.0, 6.0)
    return values.astype(jnp.bfloat16)


def draw_fine_gain(key, part):
    sub = jax.random.fold_in(key, 21)
    values = 1.0 + 0.18 * jnp.clip(jax.random.normal(sub, (D,), jnp.float32), -5.0, 5.0)
    return values.astype(jnp.float32)


def draw_parent_gain(key, part):
    sub = jax.random.fold_in(key, 22)
    values = 1.0 + 0.18 * jnp.clip(jax.random.normal(sub, (D,), jnp.float32), -5.0, 5.0)
    return values.astype(jnp.float32)


def draw_w_qkv(key, part):
    sub = jax.random.fold_in(key, 11)
    scale = D ** (-0.5)
    values = jnp.clip(jax.random.normal(sub, (D, 3 * D), jnp.float32), -4.0, 4.0) * scale
    return values.astype(jnp.bfloat16)


def draw_w_parent(key, part):
    sub = jax.random.fold_in(key, 12)
    scale = D ** (-0.5)
    values = jnp.clip(jax.random.normal(sub, (D, 2 * D), jnp.float32), -4.0, 4.0) * scale
    return values.astype(jnp.bfloat16)


def scatter_about(stream_key, shape, spread, most, held_as=jnp.bfloat16):
    return jnp.clip(spread * jax.random.normal(stream_key, shape, jnp.float32), -most, most).astype(held_as)


def setup_inputs(seed: int = 0, part: int = 0) -> dict:
    key_list = jax.random.split(jax.random.key(seed), 10)
    part_splits = jax.random.split(jax.random.fold_in(key_list[9], part), 10)
    return {
        "fine_tokens": draw_fine_tokens(jax.random.fold_in(jax.random.fold_in(key_list[9], part), 71), part),
        "parent_tokens": draw_parent_tokens(jax.random.fold_in(jax.random.fold_in(key_list[9], part), 71), part),
        "shift_table": draw_shift_table(jax.random.fold_in(key_list[9], 71), part),
        "parent_slot": draw_parent_slot(jax.random.fold_in(key_list[9], 71), part),
        "fine_gain": draw_fine_gain(jax.random.fold_in(key_list[9], 71), part),
        "parent_gain": draw_parent_gain(jax.random.fold_in(key_list[9], 71), part),
        "w_qkv": draw_w_qkv(jax.random.fold_in(key_list[9], 71), part),
        "w_parent": draw_w_parent(jax.random.fold_in(key_list[9], 71), part),
        "w_out": scatter_about(key_list[8], (2 * D, D), (2 * D) ** -0.5, 0.1875),
    }


def rms_rows(matrix, gain):
    values = matrix.astype(jnp.float32)
    factor = lax.rsqrt(lax.optimization_barrier(jnp.mean(values * values, axis=-1, keepdims=True)) + 1e-06)
    return (values * factor * gain.astype(jnp.float32)).astype(jnp.bfloat16)

def attend(queries, key_heads, value_heads):
    scores = jnp.einsum('wrhe,wshe->whrs', queries.astype(jnp.float32), key_heads.astype(jnp.float32))
    scores = scores / jnp.sqrt(jnp.float32(HD))
    highest = lax.optimization_barrier(jnp.max(scores, axis=-1, keepdims=True))
    powers = jnp.exp(scores - highest)
    weights = (powers / lax.optimization_barrier(jnp.sum(powers, axis=-1, keepdims=True))).astype(jnp.bfloat16)
    result = jnp.einsum('whrs,wshe->wrhe', weights.astype(jnp.float32), value_heads.astype(jnp.float32))
    return result.astype(jnp.bfloat16)

def reference(fine_tokens, parent_tokens, shift_table, parent_slot, fine_gain, parent_gain, w_qkv, w_parent, w_out):
    block_rows = PAR_DEV * PAR_DEV // NPAR
    stored = jnp.arange(NPAR, dtype=jnp.int32)
    owners = stored % PAR_DEV // block_rows
    target = (owners * PAR_DEV + parent_slot).astype(jnp.int32)
    parents = jnp.zeros_like(parent_tokens).at[target].set(parent_tokens)
    normed = rms_rows(fine_tokens, fine_gain)
    qkv = jnp.dot(normed, w_qkv, preferred_element_type=jnp.float32).astype(jnp.bfloat16)
    parent_kv = jnp.dot(rms_rows(parents, parent_gain), w_parent, preferred_element_type=jnp.float32).astype(jnp.bfloat16)
    window_kv = jnp.take(qkv[:, D:], shift_table, axis=0)
    per_dev = PIX_DEV // WIN
    queries = qkv[:, :D].reshape(N_PIX, per_dev, WIN, HEADS, HD)
    self_keys = window_kv[:, :D].reshape(N_PIX, per_dev, WIN, HEADS, HD)
    self_values = window_kv[:, D:].reshape(N_PIX, per_dev, WIN, HEADS, HD)
    cross_keys = parent_kv[:, :D].reshape(N_PIX, per_dev, PWIN, HEADS, HD)
    cross_values = parent_kv[:, D:].reshape(N_PIX, per_dev, PWIN, HEADS, HD)

    def one_group(pieces):
        group_q, group_k, group_v, group_pk, group_pv = pieces
        self_out = attend(group_q, group_k, group_v).reshape(PIX_DEV, D)
        cross_out = attend(group_q, group_pk, group_pv).reshape(PIX_DEV, D)
        return jnp.concatenate([self_out, cross_out], axis=1)
    joined = lax.map(one_group, (queries, self_keys, self_values, cross_keys, cross_values))
    joined = joined.reshape(NPIX, 2 * D)
    branch = jnp.dot(joined, w_out, preferred_element_type=jnp.float32)
    return (fine_tokens.astype(jnp.float32) + branch).astype(jnp.bfloat16)
```

```python
import functools
import math

import jax
import jax.numpy as jnp
from jax import lax
from jax.experimental import pallas as pl
from jax.experimental.pallas import tpu as pltpu
from jax.sharding import PartitionSpec as P

HEADS = 16
WIN = 256
HALO = 128
PWIN = 64
LANES = 128
F32 = jnp.float32
BF16 = jnp.bfloat16
VMEM = pl.BlockSpec(memory_space=pltpu.VMEM)


def mm(a, b, dims=((1,), (0,))):
    return lax.dot_general(a, b, (dims, ((), ())), preferred_element_type=F32)


def rms_rows(matrix, gain):
    values = matrix.astype(F32)
    factor = lax.rsqrt(jnp.mean(values * values, axis=-1, keepdims=True) + 1e-06)
    return (values * factor * gain).astype(BF16)


def softmax_down(scores, scale, groups):
    rows, cols = scores.shape
    scores = scores.reshape(groups, rows // groups, cols)
    highest = jnp.max(scores, axis=1, keepdims=True)
    powers = jnp.exp2((scores - highest) * scale)
    weights = powers * (1.0 / jnp.sum(powers, axis=1, keepdims=True))
    return weights.astype(BF16).reshape(rows, cols)


def column_of(row):
    wide = jnp.broadcast_to(row, (LANES, row.shape[1]))
    return jnp.concatenate(
        [wide[:, k : k + LANES].T for k in range(0, row.shape[1], LANES)], axis=0
    )


def one_hot_rows(row, base, width):
    column = column_of(row) - base
    lane = lax.broadcasted_iota(jnp.int32, column.shape, 1)
    return jnp.concatenate(
        [jnp.where(column == lane + k, 1.0, 0.0).astype(BF16) for k in range(0, width, LANES)], axis=1
    )


def self_attention(span, picks, query_t, w_kv, wv_t, head_size, store):
    features = span.shape[1]
    scale = math.log2(math.e) / math.sqrt(head_size)
    gathered = mm(picks, span).astype(BF16)
    keys = mm(gathered, w_kv[:, :features]).astype(BF16)
    values_t = mm(wv_t, gathered, ((1,), (1,))).astype(BF16)
    per_tile = LANES // head_size
    cols = query_t.shape[1]
    for head in range(features // head_size):
        tile, inside = head // per_tile, head % per_tile
        rows = query_t[head * head_size : (head + 1) * head_size]
        parts = []
        if inside:
            parts.append(jnp.zeros((inside * head_size, cols), BF16))
        parts.append(rows)
        if inside < per_tile - 1:
            parts.append(jnp.zeros(((per_tile - 1 - inside) * head_size, cols), BF16))
        scores = mm(keys[:, tile * LANES : (tile + 1) * LANES], jnp.concatenate(parts, axis=0))
        weights = softmax_down(scores, scale, 1)
        store(head, mm(values_t[head * head_size : (head + 1) * head_size], weights).astype(BF16))


def local_kernel(fine, index, gain, w_qkv, normed_out, query_out, self_out, wv_out, *, windows, head_size):
    rows, features = fine.shape
    wv_out[...] = w_qkv[:, 2 * features :].T
    wq_t = w_qkv[:, :features].T
    for w in range(windows):
        normed_out[w * WIN : (w + 1) * WIN] = rms_rows(fine[w * WIN : (w + 1) * WIN], gain[...])
    for w in range(windows):
        query_out[w] = mm(wq_t, normed_out[w * WIN : (w + 1) * WIN], ((1,), (1,))).astype(BF16)

    def window(w, carry):
        span = normed_out[pl.ds(pl.multiple_of(w * WIN - HALO, HALO), WIN + 2 * HALO)]
        picks = one_hot_rows(index[w], w * WIN, WIN + 2 * HALO)

        def store(head, value):
            self_out[w - 1, head * head_size : (head + 1) * head_size] = value

        self_attention(span, picks, query_out[w], w_qkv[:, features:], wv_out[...], head_size, store)
        return carry

    lax.fori_loop(1, windows - 1, window, 0)


def edge_kernel(
    fine, normed, query, self_in, wv_t, before, after, index, parents, slots, gain, parent_gain, w_qkv, w_parent,
    w_out, out, ends, self_all, p_keys, p_values, *, windows, head_size,
):
    rows, features = fine.shape
    span_rows = WIN + 2 * HALO
    ends[0, :HALO] = rms_rows(before[...], gain[...])
    ends[0, HALO:] = normed[: span_rows - HALO]
    ends[1, : span_rows - HALO] = normed[rows - (span_rows - HALO) :]
    ends[1, span_rows - HALO :] = rms_rows(after[...], gain[...])
    self_all[1 : windows - 1] = self_in[...]

    count = parents.shape[0]
    place = lax.broadcasted_iota(jnp.int32, (count, count), 0)
    picks = jnp.where(place == jnp.broadcast_to(slots[...], (count, count)), 1.0, 0.0).astype(BF16)
    ordered = mm(picks, parents[...]).astype(BF16)
    normed_parents = rms_rows(ordered, parent_gain[...])
    p_keys[...] = mm(normed_parents, w_parent[:, :features]).astype(BF16)
    p_values[...] = mm(normed_parents, w_parent[:, features:]).astype(BF16)

    def edge(e, carry):
        w = e * (windows - 1)
        picks = one_hot_rows(index[w], w * WIN, span_rows)

        def store(head, value):
            self_all[w, head * head_size : (head + 1) * head_size] = value

        self_attention(ends[e], picks, query[w], w_qkv[:, features:], wv_t[...], head_size, store)
        return carry

    lax.fori_loop(0, 2, edge, 0)

    scale = math.log2(math.e) / math.sqrt(head_size)
    per_tile = LANES // head_size
    lane_head = lax.broadcasted_iota(jnp.int32, (per_tile * PWIN, LANES), 1) // head_size
    row_head = lax.broadcasted_iota(jnp.int32, (per_tile * PWIN, LANES), 0) // PWIN
    own = lane_head == row_head

    def finish(w, carry):
        own_rows = pl.ds(pl.multiple_of(w * PWIN, PWIN), PWIN)
        keys, values = p_keys[own_rows], p_values[own_rows]
        crossed = []
        for tile in range(features // LANES):
            lanes = slice(tile * LANES, (tile + 1) * LANES)
            spread = jnp.where(own, jnp.concatenate([keys[:, lanes]] * per_tile, axis=0), 0)
            scores = mm(spread, query[w, lanes])
            weights = softmax_down(scores, scale, per_tile)
            spread = jnp.where(own, jnp.concatenate([values[:, lanes]] * per_tile, axis=0), 0)
            crossed.append(mm(spread, weights, ((0,), (0,))).astype(BF16))
        here = pl.ds(pl.multiple_of(w * WIN, WIN), WIN)
        branch = mm(self_all[w], w_out[:features], ((0,), (0,)))
        branch += mm(jnp.concatenate(crossed, axis=0), w_out[features:], ((0,), (0,)))
        out[here] = (fine[here].astype(F32) + branch).astype(BF16)
        return carry

    lax.fori_loop(0, windows, finish, 0)


def on_device(
    fine_tokens, parent_tokens, shift_table, parent_slot, fine_gain, parent_gain, w_qkv, w_parent, w_out,
):
    rows, features = fine_tokens.shape
    devices = lax.axis_size("pix")
    windows = rows // WIN
    head_size = features // HEADS
    offset = lax.axis_index("pix") * rows
    index = jnp.mod(shift_table - offset + HALO, rows * devices).reshape(windows, 1, WIN)
    ring = [(i, (i + 1) % devices) for i in range(devices)]
    before = lax.ppermute(fine_tokens[rows - HALO :], "pix", ring)
    after = lax.ppermute(fine_tokens[:HALO], "pix", [(j, i) for i, j in ring])
    arrived = lax.all_to_all(parent_tokens, "pix", split_axis=0, concat_axis=0, tiled=True)
    slots = lax.all_to_all(parent_slot, "pix", split_axis=0, concat_axis=0, tiled=True)
    gain = fine_gain.reshape(1, features)
    params = pltpu.CompilerParams(vmem_limit_bytes=48 * 1024 * 1024)

    normed, query, inner, wv_t = pl.pallas_call(
        functools.partial(local_kernel, windows=windows, head_size=head_size),
        out_shape=[
            jax.ShapeDtypeStruct((rows, features), BF16),
            jax.ShapeDtypeStruct((windows, features, WIN), BF16),
            jax.ShapeDtypeStruct((windows - 2, features, WIN), BF16),
            jax.ShapeDtypeStruct((features, features), BF16),
        ],
        in_specs=[VMEM] * 4,
        out_specs=[VMEM] * 4,
        compiler_params=params,
        cost_estimate=pl.CostEstimate(flops=8 * 10**9, bytes_accessed=4 * 10**6, transcendentals=2 * 10**6),
        name="local",
    )(fine_tokens, index, gain, w_qkv)

    return pl.pallas_call(
        functools.partial(edge_kernel, windows=windows, head_size=head_size),
        out_shape=jax.ShapeDtypeStruct((rows, features), BF16),
        in_specs=[VMEM] * 15,
        out_specs=VMEM,
        scratch_shapes=[
            pltpu.VMEM((2, WIN + 2 * HALO, features), BF16),
            pltpu.VMEM((windows, features, WIN), BF16),
            pltpu.VMEM((parent_tokens.shape[0], features), BF16),
            pltpu.VMEM((parent_tokens.shape[0], features), BF16),
        ],
        compiler_params=params,
        cost_estimate=pl.CostEstimate(flops=10 * 10**9, bytes_accessed=6 * 10**6, transcendentals=3 * 10**6),
        name="edges",
    )(
        fine_tokens, normed, query, inner, wv_t, before, after, index, arrived, slots.reshape(1, -1), gain,
        parent_gain.reshape(1, features), w_qkv, w_parent, w_out,
    )


def solution(mesh):
    return jax.shard_map(
        on_device,
        mesh=mesh,
        in_specs=(P(("batch", "pix"), None), P(("batch", "pix"), None), P("pix"), P("pix"), P(), P(), P(), P(), P()),
        out_specs=P(("batch", "pix"), None),
        check_vma=False,
    )
```

```python
import functools
import math

import jax
import jax.numpy as jnp
from jax import lax
from jax.experimental import pallas as pl
from jax.experimental.pallas import tpu as pltpu
from jax.sharding import PartitionSpec as P

HEADS = 16
WIN = 256
HALO = 128
PWIN = 64
LANES = 128
SPAN = WIN + 2 * HALO
F32 = jnp.float32
BF16 = jnp.bfloat16
VMEM = pl.BlockSpec(memory_space=pltpu.VMEM)
HBM = pl.BlockSpec(memory_space=pltpu.HBM)
MIB = 1024 * 1024
NN, NT, TN = ((1,), (0,)), ((1,), (1,)), ((0,), (0,))


def mm(a, b, dims=NN):
    return lax.dot_general(a, b, (dims, ((), ())), preferred_element_type=F32)


def rms_rows(matrix, gain):
    values = matrix.astype(F32)
    factor = lax.rsqrt(jnp.mean(values * values, axis=-1, keepdims=True) + 1e-06)
    return (values * factor * gain).astype(BF16)


def softmax_down(scores, scale):
    powers = jnp.exp2((scores - jnp.max(scores, axis=0, keepdims=True)) * scale)
    return (powers * (1.0 / jnp.sum(powers, axis=0, keepdims=True))).astype(BF16)


def column_of(row):
    wide = jnp.broadcast_to(row, (LANES, row.shape[1]))
    return jnp.concatenate([wide[:, k : k + LANES].T for k in range(0, row.shape[1], LANES)], axis=0)


def one_hot(column, width):
    lane = lax.broadcasted_iota(jnp.int32, column.shape, 1)
    return jnp.concatenate(
        [jnp.where(column == lane + k, 1.0, 0.0).astype(BF16) for k in range(0, width, LANES)], axis=1
    )


def spread(rows, head_size):
    lane = lax.broadcasted_iota(jnp.int32, rows.shape, 1) // head_size
    return jnp.concatenate([jnp.where(lane == k, rows, 0) for k in range(LANES // head_size)], axis=0)


def gather_kv(span, row, base, w_key, w_value):
    gathered = mm(one_hot(column_of(row) - base, SPAN), span).astype(BF16)
    return mm(gathered, w_key).astype(BF16), mm(gathered, w_value).astype(BF16).T


def self_attention(keys, values_t, query, head_size, store):
    features = query.shape[1]
    scale = math.log2(math.e) / math.sqrt(head_size)
    tiles = [slice(k, k + LANES) for k in range(0, features, LANES)]
    scores = [mm(spread(keys[:, tile], head_size), query[:, tile], NT) for tile in tiles]
    count = keys.shape[0]
    per_tile = LANES // head_size
    for head in range(features // head_size):
        part = (head % per_tile) * count
        weights = softmax_down(scores[head // per_tile][part : part + count], scale)
        store(head, mm(values_t[head * head_size : (head + 1) * head_size], weights).astype(BF16))


def cross_attention(keys, values, query, head_size):
    scale = math.log2(math.e) / math.sqrt(head_size)
    per_tile = LANES // head_size
    tiles = [slice(k, k + LANES) for k in range(0, query.shape[1], LANES)]
    scores = [mm(spread(keys[:, tile], head_size), query[:, tile], NT) for tile in tiles]
    out = []
    for tile, score in zip(tiles, scores):
        weights = [softmax_down(score[k * PWIN : (k + 1) * PWIN], scale) for k in range(per_tile)]
        out.append(mm(spread(values[:, tile], head_size), jnp.concatenate(weights, axis=0), TN).astype(BF16))
    return jnp.concatenate(out, axis=0)


def block(w, size):
    return pl.ds(pl.multiple_of(w * size, size), size)


def pack_kernel(fine, parents, slots, first, second, packed, parents_s, slots_s, sems):
    rows, features = fine.shape
    odd = lax.rem(lax.axis_index("pix"), 2)
    ends = rows - HALO
    pieces = [
        (slots, slots_s),
        (parents, parents_s),
        (fine.at[pl.ds(pl.multiple_of((1 - odd) * ends, HALO), HALO)], first),
        (fine.at[pl.ds(pl.multiple_of(odd * ends, HALO), HALO)], second),
    ]
    copies = [pltpu.make_async_copy(src, dst, sems.at[k]) for k, (src, dst) in enumerate(pieces)]
    for copy in copies:
        copy.start()
    copies[0].wait()
    packed[:, features:] = column_of(slots_s[...]).astype(F32).astype(BF16)
    copies[1].wait()
    packed[:, :features] = parents_s[...]
    copies[2].wait()
    copies[3].wait()


def local_kernel(
    fine, w_qkv, index, gain, query, inner, fine_s, w_s, index_s, gain_s, normed, query_s, inner_s, sems,
    *, windows, head_size,
):
    rows, features = fine.shape
    small = [
        pltpu.make_async_copy(gain, gain_s, sems.at[0]),
        pltpu.make_async_copy(index, index_s, sems.at[1]),
    ]
    weigh = [
        pltpu.make_async_copy(w_qkv.at[:, c * features : (c + 1) * features], w_s.at[c], sems.at[2 + c])
        for c in range(3)
    ]
    fetch = [
        pltpu.make_async_copy(fine.at[w * WIN : (w + 1) * WIN], fine_s.at[w], sems.at[5 + w]) for w in range(windows)
    ]
    for copy in small + fetch + weigh:
        copy.start()
    for copy in small:
        copy.wait()
    for w, copy in enumerate(fetch):
        copy.wait()
        normed[w * WIN : (w + 1) * WIN] = rms_rows(fine_s[w], gain_s[...])
    for copy in weigh:
        copy.wait()
    query_s[...] = mm(normed[WIN : rows - WIN], w_s[0]).astype(BF16)
    queries = pltpu.make_async_copy(query_s, query, sems.at[5 + windows])
    queries.start()

    def window(i, carry):
        w = i + 1
        span = normed[pl.ds(pl.multiple_of(w * WIN - HALO, HALO), SPAN)]
        keys, values_t = gather_kv(span, index_s[w], w * WIN, w_s[1], w_s[2])

        def store(head, value):
            inner_s[i, head * head_size : (head + 1) * head_size] = value

        self_attention(keys, values_t, query_s[block(i, WIN)], head_size, store)
        pltpu.make_async_copy(inner_s.at[i], inner.at[i], sems.at[6 + windows]).start()
        return carry

    lax.fori_loop(0, windows - 2, window, 0)
    queries.wait()
    pltpu.make_async_copy(inner_s, inner, sems.at[6 + windows]).wait()


def edge_kernel(
    fine, query, inner, first, second, index, arrived, gain, parent_gain, w_qkv, w_parent, w_out,
    out, fine_s, query_s, inner_s, near_s, index_s, arrived_s, gain_s, w_s, wp_s, wo_s,
    out_s, spans, query_e, edge_self, p_keys, p_values, sems, *, windows, head_size,
):
    rows, features = fine.shape
    pieces = [
        (gain, gain_s.at[0]),
        (parent_gain, gain_s.at[1]),
        (arrived, arrived_s),
        (first, near_s.at[0]),
        (second, near_s.at[1]),
        (index, index_s),
        (fine, fine_s),
        (w_parent, wp_s),
        (w_qkv.at[:, :features], w_s.at[0]),
        (w_qkv.at[:, features : 2 * features], w_s.at[1]),
        (w_qkv.at[:, 2 * features :], w_s.at[2]),
        (query, query_s),
        (w_out, wo_s),
        (inner, inner_s),
    ]
    fetch = [pltpu.make_async_copy(src, dst, sems.at[1 + k]) for k, (src, dst) in enumerate(pieces)]
    for copy in fetch:
        copy.start()

    for copy in fetch[:3]:
        copy.wait()
    count = arrived.shape[0]
    places = one_hot(arrived_s[:, features:].astype(F32).astype(jnp.int32), count)
    ordered = mm(places, arrived_s[:, :features], TN).astype(BF16)
    normed_parents = rms_rows(ordered, gain_s[1])
    for copy in fetch[3:7]:
        copy.wait()
    odd = lax.rem(lax.axis_index("pix"), 2) == 1
    before = jnp.where(odd, near_s[0], near_s[1])
    after = jnp.where(odd, near_s[1], near_s[0])
    spans[0, :HALO] = rms_rows(before, gain_s[0])
    spans[0, HALO:] = rms_rows(fine_s[: SPAN - HALO], gain_s[0])
    spans[1, : SPAN - HALO] = rms_rows(fine_s[rows - (SPAN - HALO) :], gain_s[0])
    spans[1, SPAN - HALO :] = rms_rows(after, gain_s[0])
    for copy in fetch[7:11]:
        copy.wait()
    p_keys[...] = mm(normed_parents, wp_s[:, :features]).astype(BF16)
    p_values[...] = mm(normed_parents, wp_s[:, features:]).astype(BF16)
    for e in range(2):
        query_e[e] = mm(spans[e, HALO : HALO + WIN], w_s[0]).astype(BF16)
    for copy in fetch[11:]:
        copy.wait()

    def finish(w, query_w, self_t):
        here = block(w, WIN)
        own = block(w, PWIN)
        crossed = cross_attention(p_keys[own], p_values[own], query_w, head_size)
        branch = mm(self_t, wo_s[:features], TN) + mm(crossed, wo_s[features:], TN)
        out_s[here] = (fine_s[here].astype(F32) + branch).astype(BF16)
        pltpu.make_async_copy(out_s.at[here], out.at[here], sems.at[0]).start()

    def between(i, carry):
        finish(i + 1, query_s[block(i, WIN)], inner_s[i])
        return carry

    def edge(e, carry):
        w = e * (windows - 1)
        keys, values_t = gather_kv(spans[e], index_s[w], w * WIN, w_s[1], w_s[2])

        def store(head, value):
            edge_self[head * head_size : (head + 1) * head_size] = value

        self_attention(keys, values_t, query_e[e], head_size, store)
        finish(w, query_e[e], edge_self[...])
        return carry

    lax.fori_loop(0, windows - 2, between, 0)
    lax.fori_loop(0, 2, edge, 0)
    pltpu.make_async_copy(out_s, out, sems.at[0]).wait()


def on_device(
    fine_tokens, parent_tokens, shift_table, parent_slot, fine_gain, parent_gain, w_qkv, w_parent, w_out,
):
    rows, features = fine_tokens.shape
    parents = parent_tokens.shape[0]
    devices = lax.axis_size("pix")
    windows = rows // WIN
    head_size = features // HEADS
    offset = lax.axis_index("pix") * rows
    index = jnp.mod(shift_table - offset + HALO, rows * devices).reshape(windows, 1, WIN)
    gain = fine_gain.reshape(1, features)

    params = pltpu.CompilerParams(vmem_limit_bytes=60 * MIB)

    def array(*shape):
        return jax.ShapeDtypeStruct(shape, BF16)

    first, second, packed = pl.pallas_call(
        pack_kernel,
        out_shape=[array(HALO, features), array(HALO, features), array(parents, features + LANES)],
        in_specs=[HBM] * 3,
        out_specs=[VMEM] * 3,
        scratch_shapes=[
            pltpu.VMEM((parents, features), BF16),
            pltpu.VMEM((1, parents), jnp.int32),
            pltpu.SemaphoreType.DMA((4,)),
        ],
        compiler_params=params,
        name="pack",
    )(fine_tokens, parent_tokens, parent_slot.reshape(1, parents))
    pairs = [(i, i + 1 - 2 * (i % 2)) for i in range(devices)]
    across = [(i, (i - 1 + 2 * (i % 2)) % devices) for i in range(devices)]
    first = lax.ppermute(first, "pix", pairs)
    second = lax.ppermute(second, "pix", across)
    arrived = lax.all_to_all(packed, "pix", split_axis=0, concat_axis=0, tiled=True)

    query, inner = pl.pallas_call(
        functools.partial(local_kernel, windows=windows, head_size=head_size),
        out_shape=[array(rows - 2 * WIN, features), array(windows - 2, features, WIN)],
        in_specs=[HBM] * 4,
        out_specs=[HBM] * 2,
        scratch_shapes=[
            pltpu.VMEM((windows, WIN, features), BF16),
            pltpu.VMEM((3, features, features), BF16),
            pltpu.VMEM((windows, 1, WIN), jnp.int32),
            pltpu.VMEM((1, features), F32),
            pltpu.VMEM((rows, features), BF16),
            pltpu.VMEM((rows - 2 * WIN, features), BF16),
            pltpu.VMEM((windows - 2, features, WIN), BF16),
            pltpu.SemaphoreType.DMA((windows + 7,)),
        ],
        compiler_params=params,
        cost_estimate=pl.CostEstimate(flops=8 * 10**9, bytes_accessed=4 * 10**6, transcendentals=2 * 10**6),
        name="local",
    )(fine_tokens, w_qkv, index, gain)

    return pl.pallas_call(
        functools.partial(edge_kernel, windows=windows, head_size=head_size),
        out_shape=array(rows, features),
        in_specs=[HBM] * 12,
        out_specs=HBM,
        scratch_shapes=[
            pltpu.VMEM((rows, features), BF16),
            pltpu.VMEM((rows - 2 * WIN, features), BF16),
            pltpu.VMEM((windows - 2, features, WIN), BF16),
            pltpu.VMEM((2, HALO, features), BF16),
            pltpu.VMEM((windows, 1, WIN), jnp.int32),
            pltpu.VMEM((parents, features + LANES), BF16),
            pltpu.VMEM((2, 1, features), F32),
            pltpu.VMEM((3, features, features), BF16),
            pltpu.VMEM((features, 2 * features), BF16),
            pltpu.VMEM((2 * features, features), BF16),
            pltpu.VMEM((rows, features), BF16),
            pltpu.VMEM((2, SPAN, features), BF16),
            pltpu.VMEM((2, WIN, features), BF16),
            pltpu.VMEM((features, WIN), BF16),
            pltpu.VMEM((parents, features), BF16),
            pltpu.VMEM((parents, features), BF16),
            pltpu.SemaphoreType.DMA((15,)),
        ],
        compiler_params=params,
        cost_estimate=pl.CostEstimate(flops=10 * 10**9, bytes_accessed=6 * 10**6, transcendentals=3 * 10**6),
        name="edges",
    )(
        fine_tokens, query, inner, first, second, index, arrived, gain, parent_gain.reshape(1, features),
        w_qkv, w_parent, w_out,
    )


def solution(mesh):
    return jax.shard_map(
        on_device,
        mesh=mesh,
        in_specs=(P(("batch", "pix"), None), P(("batch", "pix"), None), P("pix"), P("pix"), P(), P(), P(), P(), P()),
        out_specs=P(("batch", "pix"), None),
        check_vma=False,
    )
```

```python
import functools
import math

import jax
import jax.numpy as jnp
from jax import lax
from jax.experimental import pallas as pl
from jax.experimental.pallas import tpu as pltpu
from jax.sharding import PartitionSpec as P

HEADS = 16
WIN = 256
HALO = 128
PWIN = 64
LANES = 128
SPAN = WIN + 2 * HALO
F32 = jnp.float32
BF16 = jnp.bfloat16
VMEM = pl.BlockSpec(memory_space=pltpu.VMEM)
HBM = pl.BlockSpec(memory_space=pltpu.HBM)
MIB = 1024 * 1024
NN, NT, TN = ((1,), (0,)), ((1,), (1,)), ((0,), (0,))


def mm(a, b, dims=NN):
    return lax.dot_general(a, b, (dims, ((), ())), preferred_element_type=F32)


def rms_rows(matrix, gain):
    values = matrix.astype(F32)
    factor = lax.rsqrt(jnp.mean(values * values, axis=-1, keepdims=True) + 1e-06)
    return (values * factor * gain).astype(BF16)


def softmax_down(scores, scale):
    powers = jnp.exp2((scores - jnp.max(scores, axis=0, keepdims=True)) * scale)
    return (powers * (1.0 / jnp.sum(powers, axis=0, keepdims=True))).astype(BF16)


def column_of(row):
    wide = jnp.broadcast_to(row, (LANES, row.shape[1]))
    return jnp.concatenate([wide[:, k : k + LANES].T for k in range(0, row.shape[1], LANES)], axis=0)


def one_hot(column, width):
    lane = lax.broadcasted_iota(jnp.int32, column.shape, 1)
    return jnp.concatenate(
        [jnp.where(column == lane + k, 1.0, 0.0).astype(BF16) for k in range(0, width, LANES)], axis=1
    )


def spread(rows, head_size):
    lane = lax.broadcasted_iota(jnp.int32, rows.shape, 1) // head_size
    return jnp.concatenate([jnp.where(lane == k, rows, 0) for k in range(LANES // head_size)], axis=0)


def gather_kv(span, row, first_row, all_rows, w_key, w_value):
    offset = row - first_row
    offset = jnp.where(offset < 0, offset + all_rows, offset)
    offset = jnp.where(offset >= all_rows, offset - all_rows, offset)
    gathered = mm(one_hot(column_of(offset), SPAN), span).astype(BF16)
    return mm(gathered, w_key).astype(BF16), mm(gathered, w_value).astype(BF16).T


def self_attention(keys, values_t, query, head_size, store):
    features = query.shape[1]
    scale = math.log2(math.e) / math.sqrt(head_size)
    tiles = [slice(k, k + LANES) for k in range(0, features, LANES)]
    scores = [mm(spread(keys[:, tile], head_size), query[:, tile], NT) for tile in tiles]
    count = keys.shape[0]
    per_tile = LANES // head_size
    for head in range(features // head_size):
        part = (head % per_tile) * count
        weights = softmax_down(scores[head // per_tile][part : part + count], scale)
        store(head, mm(values_t[head * head_size : (head + 1) * head_size], weights).astype(BF16))


def cross_attention(keys, values, query, head_size):
    scale = math.log2(math.e) / math.sqrt(head_size)
    per_tile = LANES // head_size
    tiles = [slice(k, k + LANES) for k in range(0, query.shape[1], LANES)]
    scores = [mm(spread(keys[:, tile], head_size), query[:, tile], NT) for tile in tiles]
    out = []
    for tile, score in zip(tiles, scores):
        weights = [softmax_down(score[k * PWIN : (k + 1) * PWIN], scale) for k in range(per_tile)]
        out.append(mm(spread(values[:, tile], head_size), jnp.concatenate(weights, axis=0), TN).astype(BF16))
    return jnp.concatenate(out, axis=0)


def span_start(w, rows):
    return lax.axis_index("pix") * rows + w * WIN - HALO


def block(w, size):
    return pl.ds(pl.multiple_of(w * size, size), size)


def pack_kernel(fine, parents, slots, first, second, packed, parents_s, slots_s, column_s, sems):
    rows, features = fine.shape
    odd = lax.rem(lax.axis_index("pix"), 2)
    pieces = [
        (slots, slots_s),
        (parents, parents_s),
        (fine.at[pl.ds(pl.multiple_of((1 - odd) * (rows - HALO), HALO), HALO)], first),
        (fine.at[pl.ds(pl.multiple_of(odd * (rows - HALO), HALO), HALO)], second),
        (parents_s, packed.at[:, :features]),
        (column_s, packed.at[:, features:]),
    ]
    copies = [pltpu.make_async_copy(src, dst, sems.at[k]) for k, (src, dst) in enumerate(pieces)]
    for copy in copies[:4]:
        copy.start()
    copies[0].wait()
    column_s[...] = column_of(slots_s[...]).astype(F32).astype(BF16)
    copies[5].start()
    copies[1].wait()
    copies[4].start()
    for copy in copies[2:]:
        copy.wait()


def gate_kernel(before, held, passed):
    pass


def local_kernel(
    fine, w_qkv, index, gain, parent_gain, query, inner, fine_v, index_v, gain_v, w_v, normed, sems,
    *, windows, head_size, all_rows,
):
    rows, features = fine.shape
    pieces = [
        (gain, gain_v.at[0]),
        (parent_gain, gain_v.at[1]),
        (index, index_v),
    ]
    pieces += [(fine.at[w * WIN : (w + 1) * WIN], fine_v.at[w * WIN : (w + 1) * WIN]) for w in range(windows)]
    pieces += [(w_qkv.at[:, c * features : (c + 1) * features], w_v.at[c]) for c in range(3)]
    fetch = [pltpu.make_async_copy(src, dst, sems.at[k]) for k, (src, dst) in enumerate(pieces)]
    for copy in fetch:
        copy.start()
    for copy in fetch[:3]:
        copy.wait()
    for w in range(windows):
        fetch[3 + w].wait()
        here = slice(w * WIN, (w + 1) * WIN)
        normed[here] = rms_rows(fine_v[here], gain_v[0])
    for copy in fetch[3 + windows :]:
        copy.wait()
    query[...] = mm(normed[...], w_v[0]).astype(BF16)

    def window(i, carry):
        w = i + 1
        span = normed[pl.ds(pl.multiple_of(w * WIN - HALO, HALO), SPAN)]
        keys, values_t = gather_kv(span, index_v[w], span_start(w, rows), all_rows, w_v[1], w_v[2])

        def store(head, value):
            inner[i, head * head_size : (head + 1) * head_size] = value

        self_attention(keys, values_t, query[block(w, WIN)], head_size, store)
        return carry

    lax.fori_loop(0, windows - 2, window, 0)


def edge_kernel(
    query, fine, index, gains, first, second, w_qkv, outer, w_kv, ends, sems, *, windows, head_size, all_rows,
):
    rows, features = fine.shape
    fetch = [
        pltpu.make_async_copy(w_qkv.at[:, (1 + c) * features : (2 + c) * features], w_kv.at[c], sems.at[c])
        for c in range(2)
    ]
    for copy in fetch:
        copy.start()
    odd = lax.rem(lax.axis_index("pix"), 2) == 1
    ends[0, :HALO] = rms_rows(jnp.where(odd, first[...], second[...]), gains[0])
    ends[0, HALO:] = rms_rows(fine[: SPAN - HALO], gains[0])
    ends[1, : SPAN - HALO] = rms_rows(fine[rows - (SPAN - HALO) :], gains[0])
    ends[1, SPAN - HALO :] = rms_rows(jnp.where(odd, second[...], first[...]), gains[0])
    for copy in fetch:
        copy.wait()

    def edge(e, carry):
        w = e * (windows - 1)
        keys, values_t = gather_kv(ends[e], index[w], span_start(w, rows), all_rows, w_kv[0], w_kv[1])

        def store(head, value):
            outer[e, head * head_size : (head + 1) * head_size] = value

        self_attention(keys, values_t, query[block(w, WIN)], head_size, store)
        return carry

    lax.fori_loop(0, 2, edge, 0)


def cross_kernel(
    query, inner, outer, gains, arrived, fine_h, w_parent, w_out, out, fine, wp, wo, out_s, p_keys, p_values, sems,
    *, windows, head_size, all_rows,
):
    rows, features = fine.shape
    fetch = [
        pltpu.make_async_copy(w_parent, wp, sems.at[1]),
        pltpu.make_async_copy(w_out, wo, sems.at[2]),
        pltpu.make_async_copy(fine_h, fine, sems.at[3]),
    ]
    for copy in fetch:
        copy.start()
    count = arrived.shape[0]
    places = one_hot(arrived[:, features:].astype(F32).astype(jnp.int32), count)
    ordered = mm(places, arrived[:, :features], TN).astype(BF16)
    normed_parents = rms_rows(ordered, gains[1])
    fetch[0].wait()
    p_keys[...] = mm(normed_parents, wp[:, :features]).astype(BF16)
    p_values[...] = mm(normed_parents, wp[:, features:]).astype(BF16)
    for copy in fetch[1:]:
        copy.wait()

    def finish(w, self_t):
        here = block(w, WIN)
        own = block(w, PWIN)
        crossed = cross_attention(p_keys[own], p_values[own], query[here], head_size)
        branch = mm(self_t, wo[:features], TN) + mm(crossed, wo[features:], TN)
        out_s[here] = (fine[here].astype(F32) + branch).astype(BF16)
        pltpu.make_async_copy(out_s.at[here], out.at[here], sems.at[0]).start()

    def between(i, carry):
        finish(i + 1, inner[i])
        return carry

    def edge(e, carry):
        finish(e * (windows - 1), outer[e])
        return carry

    lax.fori_loop(0, 2, edge, 0)
    lax.fori_loop(0, windows - 2, between, 0)
    pltpu.make_async_copy(out_s, out, sems.at[0]).wait()


def on_device(
    fine_tokens, parent_tokens, shift_table, parent_slot, fine_gain, parent_gain, w_qkv, w_parent, w_out,
):
    rows, features = fine_tokens.shape
    parents = parent_tokens.shape[0]
    devices = lax.axis_size("pix")
    windows = rows // WIN
    sizes = dict(windows=windows, head_size=features // HEADS, all_rows=rows * devices)
    params = pltpu.CompilerParams(vmem_limit_bytes=32 * MIB)
    semaphores = pltpu.SemaphoreType.DMA

    def near(*shape, dtype=BF16):
        return pltpu.VMEM(shape, dtype)

    def far(x):
        return pltpu.with_memory_space_constraint(x, pltpu.HBM)

    fine, weights = far(fine_tokens), far(w_qkv)
    first, second, packed = pl.pallas_call(
        pack_kernel,
        out_shape=[near(HALO, features), near(HALO, features), pltpu.HBM((parents, features + LANES), BF16)],
        in_specs=[HBM] * 3,
        out_specs=[VMEM, VMEM, HBM],
        scratch_shapes=[
            near(parents, features),
            near(1, parents, dtype=jnp.int32),
            near(parents, LANES),
            semaphores((6,)),
        ],
        compiler_params=params,
        name="pack",
    )(fine, far(parent_tokens), far(parent_slot.reshape(1, parents)))
    pairs = [(i, i + 1 - 2 * (i % 2)) for i in range(devices)]
    across = [(i, (i - 1 + 2 * (i % 2)) % devices) for i in range(devices)]
    first_in = lax.ppermute(first, "pix", pairs)
    second_in = lax.ppermute(second, "pix", across)
    packed = pl.pallas_call(
        gate_kernel,
        out_shape=pltpu.HBM((parents, features + LANES), BF16),
        in_specs=[VMEM, HBM],
        out_specs=HBM,
        input_output_aliases={1: 0},
        compiler_params=params,
        name="gate",
    )(second, far(packed))
    arrived = lax.all_to_all(packed, "pix", split_axis=0, concat_axis=0, tiled=True)

    query, inner, fine_v, index, gains = pl.pallas_call(
        functools.partial(local_kernel, **sizes),
        out_shape=[
            near(rows, features),
            near(windows - 2, features, WIN),
            near(rows, features),
            near(windows, 1, WIN, dtype=jnp.int32),
            near(2, 1, features, dtype=F32),
        ],
        in_specs=[HBM] * 5,
        out_specs=[VMEM] * 5,
        scratch_shapes=[near(3, features, features), near(rows, features), semaphores((windows + 6,))],
        compiler_params=params,
        cost_estimate=pl.CostEstimate(flops=8 * 10**9, bytes_accessed=4 * 10**6, transcendentals=2 * 10**6),
        name="local",
    )(
        fine, weights, far(shift_table.reshape(windows, 1, WIN)), far(fine_gain.reshape(1, features)),
        far(parent_gain.reshape(1, features)),
    )

    outer = pl.pallas_call(
        functools.partial(edge_kernel, **sizes),
        out_shape=near(2, features, WIN),
        in_specs=[VMEM] * 6 + [HBM],
        out_specs=VMEM,
        scratch_shapes=[near(2, features, features), near(2, SPAN, features), semaphores((2,))],
        compiler_params=params,
        cost_estimate=pl.CostEstimate(flops=8 * 10**9, bytes_accessed=2 * 10**6, transcendentals=2 * 10**6),
        name="edges",
    )(query, fine_v, index, gains, first_in, second_in, weights)

    return pl.pallas_call(
        functools.partial(cross_kernel, **sizes),
        out_shape=pltpu.HBM((rows, features), BF16),
        in_specs=[VMEM] * 5 + [HBM] * 3,
        out_specs=HBM,
        scratch_shapes=[
            near(rows, features),
            near(features, 2 * features),
            near(2 * features, features),
            near(rows, features),
            near(parents, features),
            near(parents, features),
            semaphores((4,)),
        ],
        compiler_params=params,
        cost_estimate=pl.CostEstimate(flops=5 * 10**9, bytes_accessed=6 * 10**6, transcendentals=10**6),
        name="cross",
    )(query, inner, outer, gains, arrived, fine, far(w_parent), far(w_out))


def solution(mesh):
    return jax.shard_map(
        on_device,
        mesh=mesh,
        in_specs=(P(("batch", "pix"), None), P(("batch", "pix"), None), P("pix"), P("pix"), P(), P(), P(), P(), P()),
        out_specs=P(("batch", "pix"), None),
        check_vma=False,
    )
```

```python
import functools
import math

import jax
import jax.numpy as jnp
from jax import lax
from jax.experimental import pallas as pl
from jax.experimental.pallas import tpu as pltpu
from jax.sharding import PartitionSpec as P

HEADS = 16
WIN = 256
HALO = 128
PWIN = 64
LANES = 128
SPAN = WIN + 2 * HALO
F32 = jnp.float32
BF16 = jnp.bfloat16
VMEM = pl.BlockSpec(memory_space=pltpu.VMEM)
HBM = pl.BlockSpec(memory_space=pltpu.HBM)
MIB = 1024 * 1024
NN, NT, TN = ((1,), (0,)), ((1,), (1,)), ((0,), (0,))


def mm(a, b, dims=NN):
    return lax.dot_general(a, b, (dims, ((), ())), preferred_element_type=F32)


def rms_rows(matrix, gain):
    values = matrix.astype(F32)
    factor = lax.rsqrt(jnp.mean(values * values, axis=-1, keepdims=True) + 1e-06)
    return (values * factor * gain).astype(BF16)


def softmax_down(scores, scale):
    powers = jnp.exp2((scores - jnp.max(scores, axis=0, keepdims=True)) * scale)
    return (powers * (1.0 / jnp.sum(powers, axis=0, keepdims=True))).astype(BF16)


def column_of(row):
    wide = jnp.broadcast_to(row, (LANES, row.shape[1]))
    return jnp.concatenate([wide[:, k : k + LANES].T for k in range(0, row.shape[1], LANES)], axis=0)


def one_hot(column, width):
    lane = lax.broadcasted_iota(jnp.int32, column.shape, 1)
    return jnp.concatenate(
        [jnp.where(column == lane + k, 1.0, 0.0).astype(BF16) for k in range(0, width, LANES)], axis=1
    )


def spread(rows, head_size):
    lane = lax.broadcasted_iota(jnp.int32, rows.shape, 1) // head_size
    return jnp.concatenate([jnp.where(lane == k, rows, 0) for k in range(LANES // head_size)], axis=0)


def gather(span, row, first_row, all_rows):
    offset = row - first_row
    offset = jnp.where(offset < 0, offset + all_rows, offset)
    offset = jnp.where(offset >= all_rows, offset - all_rows, offset)
    return mm(one_hot(column_of(offset), SPAN), span).astype(BF16)


def project_kv(gathered, w_kv, keys, values_t):
    keys[...] = mm(gathered[...], w_kv[0]).astype(BF16)
    values = mm(gathered[...], w_kv[1]).astype(BF16)
    for i in range(values_t.shape[0]):
        values_t[i] = values[i * WIN : (i + 1) * WIN].T


def self_attention(keys, values_t, query, head_size, store):
    features = query.shape[1]
    scale = math.log2(math.e) / math.sqrt(head_size)
    tiles = [slice(k, k + LANES) for k in range(0, features, LANES)]
    scores = [mm(spread(keys[:, tile], head_size), query[:, tile], NT) for tile in tiles]
    count = keys.shape[0]
    per_tile = LANES // head_size
    for head in range(features // head_size):
        part = (head % per_tile) * count
        weights = softmax_down(scores[head // per_tile][part : part + count], scale)
        store(head, mm(values_t[head * head_size : (head + 1) * head_size], weights).astype(BF16))


def cross_attention(keys, values, query, head_size):
    scale = math.log2(math.e) / math.sqrt(head_size)
    per_tile = LANES // head_size
    tiles = [slice(k, k + LANES) for k in range(0, query.shape[1], LANES)]
    scores = [mm(spread(keys[:, tile], head_size), query[:, tile], NT) for tile in tiles]
    out = []
    for tile, score in zip(tiles, scores):
        weights = [softmax_down(score[k * PWIN : (k + 1) * PWIN], scale) for k in range(per_tile)]
        out.append(mm(spread(values[:, tile], head_size), jnp.concatenate(weights, axis=0), TN).astype(BF16))
    return jnp.concatenate(out, axis=0)


def span_start(w, rows):
    return lax.axis_index("pix") * rows + w * WIN - HALO


def block(w, size):
    return pl.ds(pl.multiple_of(w * size, size), size)


def pack_kernel(
    fine, parents, slots, index, gain, parent_gain, w_qkv, first, second, packed, normed, index_v, gains, w_q,
    fine_s, parents_s, slots_s, column_s, sems, *, windows,
):
    rows, features = fine.shape
    odd = lax.rem(lax.axis_index("pix"), 2)
    pieces = [
        (slots, slots_s),
        (parents, parents_s),
        (fine.at[pl.ds(pl.multiple_of((1 - odd) * (rows - HALO), HALO), HALO)], first),
        (fine.at[pl.ds(pl.multiple_of(odd * (rows - HALO), HALO), HALO)], second),
        (gain, gains.at[0]),
        (parent_gain, gains.at[1]),
        (index, index_v),
    ]
    blocks = [slice(w * WIN, (w + 1) * WIN) for w in range(windows)]
    pieces += [(fine.at[here], fine_s.at[here]) for here in blocks]
    weigh = pltpu.make_async_copy(w_qkv.at[:, :features], w_q, sems.at[9 + windows])
    pieces += [(parents_s, packed.at[:, :features]), (column_s, packed.at[:, features:])]
    copies = [pltpu.make_async_copy(src, dst, sems.at[k]) for k, (src, dst) in enumerate(pieces)]
    for copy in copies[:-2] + [weigh]:
        copy.start()
    copies[0].wait()
    column_s[...] = column_of(slots_s[...]).astype(F32).astype(BF16)
    copies[-1].start()
    copies[1].wait()
    copies[-2].start()
    for copy in copies[2:7]:
        copy.wait()
    for here, copy in zip(blocks, copies[7:]):
        copy.wait()
        normed[here] = rms_rows(fine_s[here], gains[0])
    for copy in copies[-2:] + [weigh]:
        copy.wait()


def gate_kernel(before, held, passed):
    pass


def attend_windows(query, keys, values_t, out, head_size):
    def window(i, carry):
        def store(head, value):
            out[i, head * head_size : (head + 1) * head_size] = value

        self_attention(keys[block(i, WIN)], values_t[i], query(i), head_size, store)
        return carry

    lax.fori_loop(0, out.shape[0], window, 0, unroll=True)


def self_kernel(
    normed, index, gains, w_q, first, second, w_qkv, query_h, self_t, w_kv, query, ends, gathered, keys, values_t, sems,
    *, windows, head_size, all_rows,
):
    rows, features = normed.shape
    own = SPAN - HALO
    fetch = [
        pltpu.make_async_copy(w_qkv.at[:, (1 + c) * features : (2 + c) * features], w_kv.at[c], sems.at[c])
        for c in range(2)
    ]
    for copy in fetch:
        copy.start()
    odd = lax.rem(lax.axis_index("pix"), 2) == 1
    ends[0, :HALO] = rms_rows(jnp.where(odd, first[...], second[...]), gains[0])
    ends[0, HALO:] = normed[:own]
    ends[1, :own] = normed[rows - own :]
    ends[1, own:] = rms_rows(jnp.where(odd, second[...], first[...]), gains[0])

    def pick(w, span):
        gathered[block(w, WIN)] = gather(span, index[w], span_start(w, rows), all_rows)

    def pick_inner(w, carry):
        pick(w, normed[pl.ds(pl.multiple_of(w * WIN - HALO, HALO), SPAN)])
        return carry

    pick(0, ends[0])
    pick(windows - 1, ends[1])
    lax.fori_loop(1, windows - 1, pick_inner, 0)
    query[...] = mm(normed[...], w_q[...]).astype(BF16)
    leave = pltpu.make_async_copy(query, query_h, sems.at[2])
    leave.start()
    for copy in fetch:
        copy.wait()
    project_kv(gathered, w_kv, keys, values_t)
    attend_windows(lambda w: query[block(w, WIN)], keys, values_t, self_t, head_size)
    leave.wait()


def cross_kernel(
    self_t, gains, arrived, query_h, fine_h, w_parent, w_out, out, query, fine, wp, wo, out_s, p_keys, p_values, sems,
    *, windows, head_size, all_rows,
):
    rows, features = fine.shape
    fetch = [
        pltpu.make_async_copy(w_parent, wp, sems.at[1]),
        pltpu.make_async_copy(query_h, query, sems.at[4]),
        pltpu.make_async_copy(w_out, wo, sems.at[2]),
        pltpu.make_async_copy(fine_h, fine, sems.at[3]),
    ]
    for copy in fetch:
        copy.start()
    count = arrived.shape[0]
    places = one_hot(arrived[:, features:].astype(F32).astype(jnp.int32), count)
    ordered = mm(places, arrived[:, :features], TN).astype(BF16)
    normed_parents = rms_rows(ordered, gains[1])
    fetch[0].wait()
    p_keys[...] = mm(normed_parents, wp[:, :features]).astype(BF16)
    p_values[...] = mm(normed_parents, wp[:, features:]).astype(BF16)
    for copy in fetch[1:]:
        copy.wait()

    def finish(w, carry):
        here = block(w, WIN)
        own = block(w, PWIN)
        crossed = cross_attention(p_keys[own], p_values[own], query[here], head_size)
        joined = jnp.concatenate([self_t[w], crossed], axis=0).T
        branch = mm(joined, wo[...])
        out_s[here] = (fine[here].astype(F32) + branch).astype(BF16)
        pltpu.make_async_copy(out_s.at[here], out.at[here], sems.at[0]).start()
        return carry

    lax.fori_loop(0, windows, finish, 0, unroll=True)
    pltpu.make_async_copy(out_s, out, sems.at[0]).wait()


def on_device(
    fine_tokens, parent_tokens, shift_table, parent_slot, fine_gain, parent_gain, w_qkv, w_parent, w_out,
):
    rows, features = fine_tokens.shape
    parents = parent_tokens.shape[0]
    devices = lax.axis_size("pix")
    windows = rows // WIN
    sizes = dict(windows=windows, head_size=features // HEADS, all_rows=rows * devices)
    params = pltpu.CompilerParams(vmem_limit_bytes=32 * MIB)
    semaphores = pltpu.SemaphoreType.DMA

    def near(*shape, dtype=BF16):
        return pltpu.VMEM(shape, dtype)

    def far(x):
        return pltpu.with_memory_space_constraint(x, pltpu.HBM)

    fine, weights = far(fine_tokens), far(w_qkv)
    first, second, packed, normed, index, gains, w_q = pl.pallas_call(
        functools.partial(pack_kernel, windows=windows),
        out_shape=[
            near(HALO, features),
            near(HALO, features),
            pltpu.HBM((parents, features + LANES), BF16),
            near(rows, features),
            near(windows, 1, WIN, dtype=jnp.int32),
            near(2, 1, features, dtype=F32),
            near(features, features),
        ],
        in_specs=[HBM] * 7,
        out_specs=[VMEM, VMEM, HBM] + [VMEM] * 4,
        scratch_shapes=[
            near(rows, features),
            near(parents, features),
            near(1, parents, dtype=jnp.int32),
            near(parents, LANES),
            semaphores((windows + 10,)),
        ],
        compiler_params=params,
        name="pack",
    )(
        fine, far(parent_tokens), far(parent_slot.reshape(1, parents)), far(shift_table.reshape(windows, 1, WIN)),
        far(fine_gain.reshape(1, features)), far(parent_gain.reshape(1, features)), weights,
    )
    pairs = [(i, i + 1 - 2 * (i % 2)) for i in range(devices)]
    across = [(i, (i - 1 + 2 * (i % 2)) % devices) for i in range(devices)]
    first_in = lax.ppermute(first, "pix", pairs)
    second_in = lax.ppermute(second, "pix", across)
    packed = pl.pallas_call(
        gate_kernel,
        out_shape=pltpu.HBM((parents, features + LANES), BF16),
        in_specs=[VMEM, HBM],
        out_specs=HBM,
        input_output_aliases={1: 0},
        compiler_params=params,
        name="gate",
    )(second, far(packed))
    arrived = lax.all_to_all(packed, "pix", split_axis=0, concat_axis=0, tiled=True)

    query, self_t = pl.pallas_call(
        functools.partial(self_kernel, **sizes),
        out_shape=[pltpu.HBM((rows, features), BF16), near(windows, features, WIN)],
        in_specs=[VMEM] * 6 + [HBM],
        out_specs=[HBM, VMEM],
        scratch_shapes=[
            near(2, features, features),
            near(rows, features),
            near(2, SPAN, features),
            near(rows, features),
            near(rows, features),
            near(windows, features, WIN),
            semaphores((3,)),
        ],
        compiler_params=params,
        cost_estimate=pl.CostEstimate(flops=16 * 10**9, bytes_accessed=4 * 10**6, transcendentals=4 * 10**6),
        name="self",
    )(normed, index, gains, w_q, first_in, second_in, weights)

    return pl.pallas_call(
        functools.partial(cross_kernel, **sizes),
        out_shape=pltpu.HBM((rows, features), BF16),
        in_specs=[VMEM] * 3 + [HBM] * 4,
        out_specs=HBM,
        scratch_shapes=[
            near(rows, features),
            near(rows, features),
            near(features, 2 * features),
            near(2 * features, features),
            near(rows, features),
            near(parents, features),
            near(parents, features),
            semaphores((5,)),
        ],
        compiler_params=params,
        cost_estimate=pl.CostEstimate(flops=5 * 10**9, bytes_accessed=6 * 10**6, transcendentals=10**6),
        name="cross",
    )(self_t, gains, arrived, far(query), fine, far(w_parent), far(w_out))


def solution(mesh):
    return jax.shard_map(
        on_device,
        mesh=mesh,
        in_specs=(P(("batch", "pix"), None), P(("batch", "pix"), None), P("pix"), P("pix"), P(), P(), P(), P(), P()),
        out_specs=P(("batch", "pix"), None),
        check_vma=False,
    )
```

```python
import functools
import math

import jax
import jax.numpy as jnp
from jax import lax
from jax.experimental import pallas as pl
from jax.experimental.pallas import tpu as pltpu
from jax.sharding import PartitionSpec as P

HEADS = 16
WIN = 256
HALO = 128
PWIN = 64
LANES = 128
SPAN = WIN + 2 * HALO
F32 = jnp.float32
BF16 = jnp.bfloat16
VMEM = pl.BlockSpec(memory_space=pltpu.VMEM)
HBM = pl.BlockSpec(memory_space=pltpu.HBM)
MIB = 1024 * 1024
NN, NT, TN = ((1,), (0,)), ((1,), (1,)), ((0,), (0,))


def mm(a, b, dims=NN):
    return lax.dot_general(a, b, (dims, ((), ())), preferred_element_type=F32)


def rms_rows(matrix, gain):
    values = matrix.astype(F32)
    factor = lax.rsqrt(jnp.mean(values * values, axis=-1, keepdims=True) + 1e-06)
    return (values * factor * gain).astype(BF16)


def softmax_down(scores, scale):
    powers = jnp.exp2((scores - jnp.max(scores, axis=0, keepdims=True)) * scale)
    return (powers * (1.0 / jnp.sum(powers, axis=0, keepdims=True))).astype(BF16)


def column_of(row):
    wide = jnp.broadcast_to(row, (LANES, row.shape[1]))
    return jnp.concatenate([wide[:, k : k + LANES].T for k in range(0, row.shape[1], LANES)], axis=0)


def one_hot(column, width):
    lane = lax.broadcasted_iota(jnp.int32, column.shape, 1)
    return jnp.concatenate(
        [jnp.where(column == lane + k, 1.0, 0.0).astype(BF16) for k in range(0, width, LANES)], axis=1
    )


def spread(rows, head_size):
    lane = lax.broadcasted_iota(jnp.int32, rows.shape, 1) // head_size
    return jnp.concatenate([jnp.where(lane == k, rows, 0) for k in range(LANES // head_size)], axis=0)


def gather(span, row, first_row, all_rows):
    offset = row - first_row
    offset = jnp.where(offset < 0, offset + all_rows, offset)
    offset = jnp.where(offset >= all_rows, offset - all_rows, offset)
    return mm(one_hot(column_of(offset), SPAN), span).astype(BF16)


def project_kv(gathered, w_kv, keys, values_t):
    keys[...] = mm(gathered[...], w_kv[0]).astype(BF16)
    values = mm(gathered[...], w_kv[1]).astype(BF16)
    for i in range(values_t.shape[0]):
        values_t[i] = values[i * WIN : (i + 1) * WIN].T


def self_scores(keys, query, tile, head_size):
    lanes = slice(tile * LANES, (tile + 1) * LANES)
    return mm(spread(keys[:, lanes], head_size), query[:, lanes], NT)


def self_attention(pending, following, values_t, head_size, store):
    scale = math.log2(math.e) / math.sqrt(head_size)
    per_tile = LANES // head_size
    coming = []
    for tile, scores in enumerate(pending):
        if following is not None:
            coming.append(following(tile))
        count = scores.shape[0] // per_tile
        for k in range(per_tile):
            head = tile * per_tile + k
            weights = softmax_down(scores[k * count : (k + 1) * count], scale)
            store(head, mm(values_t[head * head_size : (head + 1) * head_size], weights).astype(BF16))
    return coming


def cross_attention(keys, values, query, head_size):
    scale = math.log2(math.e) / math.sqrt(head_size)
    per_tile = LANES // head_size
    tiles = [slice(k, k + LANES) for k in range(0, query.shape[1], LANES)]
    scores = [mm(spread(keys[:, tile], head_size), query[:, tile], NT) for tile in tiles]
    out = []
    for tile, score in zip(tiles, scores):
        weights = [softmax_down(score[k * PWIN : (k + 1) * PWIN], scale) for k in range(per_tile)]
        out.append(mm(spread(values[:, tile], head_size), jnp.concatenate(weights, axis=0), TN).astype(BF16))
    return jnp.concatenate(out, axis=0)


def span_start(w, rows):
    return lax.axis_index("pix") * rows + w * WIN - HALO


def block(w, size):
    return pl.ds(pl.multiple_of(w * size, size), size)


def pack_kernel(
    fine, parents, slots, index, gain, parent_gain, first, second, packed, normed, index_v, gains,
    fine_s, parents_s, slots_s, column_s, sems, *, windows,
):
    rows, features = fine.shape
    odd = lax.rem(lax.axis_index("pix"), 2)
    pieces = [
        (slots, slots_s),
        (parents, parents_s),
        (fine.at[pl.ds(pl.multiple_of((1 - odd) * (rows - HALO), HALO), HALO)], first),
        (fine.at[pl.ds(pl.multiple_of(odd * (rows - HALO), HALO), HALO)], second),
        (gain, gains.at[0]),
        (parent_gain, gains.at[1]),
        (index, index_v),
    ]
    blocks = [slice(w * WIN, (w + 1) * WIN) for w in range(windows)]
    pieces += [(fine.at[here], fine_s.at[here]) for here in blocks]
    pieces += [(parents_s, packed.at[:, :features]), (column_s, packed.at[:, features:])]
    copies = [pltpu.make_async_copy(src, dst, sems.at[k]) for k, (src, dst) in enumerate(pieces)]
    for copy in copies[:-2]:
        copy.start()
    copies[0].wait()
    column_s[...] = column_of(slots_s[...]).astype(F32).astype(BF16)
    copies[-1].start()
    copies[1].wait()
    copies[-2].start()
    for copy in copies[2:7]:
        copy.wait()
    for here, copy in zip(blocks, copies[7:]):
        copy.wait()
        normed[here] = rms_rows(fine_s[here], gains[0])
    for copy in copies[-2:]:
        copy.wait()


def gate_kernel(before, held, passed):
    pass


def self_kernel(
    normed, index, gains, first, second, w_qkv, w_parent, query, early_h, late, wp, w_q, w_kv, early, ends, gathered, keys,
    values_t, sems,
    *, windows, head_size, all_rows,
):
    rows, features = normed.shape
    own = SPAN - HALO
    fetch = [
        pltpu.make_async_copy(w_qkv.at[:, c * features : (c + 1) * features], to, sems.at[c])
        for c, to in enumerate([w_q, w_kv.at[0], w_kv.at[1]])
    ]
    for copy in fetch:
        copy.start()
    odd = lax.rem(lax.axis_index("pix"), 2) == 1
    ends[0, :HALO] = rms_rows(jnp.where(odd, first[...], second[...]), gains[0])
    ends[0, HALO:] = normed[:own]
    ends[1, :own] = normed[rows - own :]
    ends[1, own:] = rms_rows(jnp.where(odd, second[...], first[...]), gains[0])

    def pick(w, span):
        gathered[block(w, WIN)] = gather(span, index[w], span_start(w, rows), all_rows)

    def pick_inner(w, carry):
        pick(w, normed[pl.ds(pl.multiple_of(w * WIN - HALO, HALO), SPAN)])
        return carry

    pick(0, ends[0])
    pick(windows - 1, ends[1])
    lax.fori_loop(1, windows - 1, pick_inner, 0)
    fetch[0].wait()
    query[...] = mm(normed[...], w_q[...]).astype(BF16)
    for copy in fetch[1:]:
        copy.wait()
    project_kv(gathered, w_kv, keys, values_t)
    leave = [
        pltpu.make_async_copy(
            w_parent.at[:, c * features : (c + 1) * features], wp.at[c * features : (c + 1) * features], sems.at[3 + c]
        )
        for c in range(2)
    ]
    for copy in leave:
        copy.start()
    split = early.shape[0]

    def scores(w):
        here = slice(w * WIN, (w + 1) * WIN)
        return lambda tile: self_scores(keys[here], query[here], tile, head_size)

    pending = [scores(0)(tile) for tile in range(features // LANES)]
    for w in range(windows):
        out = early.at[w] if w < split else late.at[w - split]

        def store(head, value):
            out[head * head_size : (head + 1) * head_size] = value

        following = scores(w + 1) if w + 1 < windows else None
        pending = self_attention(pending, following, values_t[w], head_size, store)
        if w < split:
            leave.append(pltpu.make_async_copy(out, early_h.at[w], sems.at[5 + w]))
            leave[-1].start()
    for copy in leave:
        copy.wait()


def cross_kernel(
    query, late, gains, arrived, wp, early_h, fine_h, w_out, out, early, fine, wo, out_s, p_keys, p_values, sems,
    *, windows, head_size, all_rows,
):
    rows, features = fine.shape
    fetch = [
        pltpu.make_async_copy(early_h, early, sems.at[1]),
        pltpu.make_async_copy(w_out, wo, sems.at[2]),
        pltpu.make_async_copy(fine_h, fine, sems.at[3]),
    ]
    for copy in fetch:
        copy.start()
    count = arrived.shape[0]
    places = one_hot(arrived[:, features:].astype(F32).astype(jnp.int32), count)
    ordered = mm(places, arrived[:, :features], TN).astype(BF16)
    normed_parents = rms_rows(ordered, gains[1])
    p_keys[...] = mm(normed_parents, wp[:features]).astype(BF16)
    p_values[...] = mm(normed_parents, wp[features:]).astype(BF16)
    split = early.shape[0]
    rows_of = [slice(w * WIN, (w + 1) * WIN) for w in range(windows)]

    def crossed(w):
        own = slice(w * PWIN, (w + 1) * PWIN)
        return cross_attention(p_keys[own], p_values[own], query[rows_of[w]], head_size)

    ahead = [crossed(w) for w in range(2)]
    for copy in fetch:
        copy.wait()
    for w, here in enumerate(rows_of):
        self_t = early[w] if w < split else late[w - split]
        joined = jnp.concatenate([self_t, ahead.pop(0)], axis=0).T
        branch = mm(joined, wo[...])
        out_s[here] = (fine[here].astype(F32) + branch).astype(BF16)
        pltpu.make_async_copy(out_s.at[here], out.at[here], sems.at[0]).start()
        if w + 2 < windows:
            ahead.append(crossed(w + 2))
    pltpu.make_async_copy(out_s, out, sems.at[0]).wait()


def on_device(
    fine_tokens, parent_tokens, shift_table, parent_slot, fine_gain, parent_gain, w_qkv, w_parent, w_out,
):
    rows, features = fine_tokens.shape
    parents = parent_tokens.shape[0]
    devices = lax.axis_size("pix")
    windows = rows // WIN
    sizes = dict(windows=windows, head_size=features // HEADS, all_rows=rows * devices)
    params = pltpu.CompilerParams(vmem_limit_bytes=32 * MIB)
    semaphores = pltpu.SemaphoreType.DMA

    def near(*shape, dtype=BF16):
        return pltpu.VMEM(shape, dtype)

    def far(x):
        return pltpu.with_memory_space_constraint(x, pltpu.HBM)

    fine, weights = far(fine_tokens), far(w_qkv)
    first, second, packed, normed, index, gains = pl.pallas_call(
        functools.partial(pack_kernel, windows=windows),
        out_shape=[
            near(HALO, features),
            near(HALO, features),
            pltpu.HBM((parents, features + LANES), BF16),
            near(rows, features),
            near(windows, 1, WIN, dtype=jnp.int32),
            near(2, 1, features, dtype=F32),
        ],
        in_specs=[HBM] * 6,
        out_specs=[VMEM, VMEM, HBM] + [VMEM] * 3,
        scratch_shapes=[
            near(rows, features),
            near(parents, features),
            near(1, parents, dtype=jnp.int32),
            near(parents, LANES),
            semaphores((windows + 9,)),
        ],
        compiler_params=params,
        name="pack",
    )(
        fine, far(parent_tokens), far(parent_slot.reshape(1, parents)), far(shift_table.reshape(windows, 1, WIN)),
        far(fine_gain.reshape(1, features)), far(parent_gain.reshape(1, features)),
    )
    pairs = [(i, i + 1 - 2 * (i % 2)) for i in range(devices)]
    across = [(i, (i - 1 + 2 * (i % 2)) % devices) for i in range(devices)]
    first_in = lax.ppermute(first, "pix", pairs)
    second_in = lax.ppermute(second, "pix", across)
    packed = pl.pallas_call(
        gate_kernel,
        out_shape=pltpu.HBM((parents, features + LANES), BF16),
        in_specs=[VMEM, HBM],
        out_specs=HBM,
        input_output_aliases={1: 0},
        compiler_params=params,
        name="gate",
    )(second, far(packed))
    arrived = lax.all_to_all(packed, "pix", split_axis=0, concat_axis=0, tiled=True)

    split = windows // 2
    query, early, late, wp = pl.pallas_call(
        functools.partial(self_kernel, **sizes),
        out_shape=[
            near(rows, features),
            pltpu.HBM((split, features, WIN), BF16),
            near(windows - split, features, WIN),
            near(2 * features, features),
        ],
        in_specs=[VMEM] * 5 + [HBM] * 2,
        out_specs=[VMEM, HBM, VMEM, VMEM],
        input_output_aliases={0: 3} if rows == 2 * features else {},
        scratch_shapes=[
            near(features, features),
            near(2, features, features),
            near(split, features, WIN),
            near(2, SPAN, features),
            near(rows, features),
            near(rows, features),
            near(windows, features, WIN),
            semaphores((5 + split,)),
        ],
        compiler_params=params,
        cost_estimate=pl.CostEstimate(flops=16 * 10**9, bytes_accessed=4 * 10**6, transcendentals=4 * 10**6),
        name="self",
    )(normed, index, gains, first_in, second_in, weights, far(w_parent))

    return pl.pallas_call(
        functools.partial(cross_kernel, **sizes),
        out_shape=pltpu.HBM((rows, features), BF16),
        in_specs=[VMEM] * 5 + [HBM] * 3,
        out_specs=HBM,
        scratch_shapes=[
            near(split, features, WIN),
            near(rows, features),
            near(2 * features, features),
            near(rows, features),
            near(parents, features),
            near(parents, features),
            semaphores((4,)),
        ],
        compiler_params=params,
        cost_estimate=pl.CostEstimate(flops=5 * 10**9, bytes_accessed=6 * 10**6, transcendentals=10**6),
        name="cross",
    )(query, late, gains, arrived, wp, far(early), fine, far(w_out))


def solution(mesh):
    return jax.shard_map(
        on_device,
        mesh=mesh,
        in_specs=(P(("batch", "pix"), None), P(("batch", "pix"), None), P("pix"), P("pix"), P(), P(), P(), P(), P()),
        out_specs=P(("batch", "pix"), None),
        check_vma=False,
    )
```

```python
import functools
import math

import jax
import jax.numpy as jnp
from jax import lax
from jax.experimental import pallas as pl
from jax.experimental.pallas import tpu as pltpu
from jax.sharding import PartitionSpec as P

HEADS = 16
WIN = 256
HALO = 128
PWIN = 64
LANES = 128
SPAN = WIN + 2 * HALO
F32 = jnp.float32
BF16 = jnp.bfloat16
VMEM = pl.BlockSpec(memory_space=pltpu.VMEM)
HBM = pl.BlockSpec(memory_space=pltpu.HBM)
MIB = 1024 * 1024
NN, NT, TN = ((1,), (0,)), ((1,), (1,)), ((0,), (0,))


def mm(a, b, dims=NN):
    return lax.dot_general(a, b, (dims, ((), ())), preferred_element_type=F32)


def rms_rows(matrix, gain):
    values = matrix.astype(F32)
    factor = lax.rsqrt(jnp.mean(values * values, axis=-1, keepdims=True) + 1e-06)
    return (values * factor * gain).astype(BF16)


def softmax_down(scores, scale):
    powers = jnp.exp2((scores - jnp.max(scores, axis=0, keepdims=True)) * scale)
    return (powers * (1.0 / jnp.sum(powers, axis=0, keepdims=True))).astype(BF16)


def column_of(row):
    wide = jnp.broadcast_to(row, (LANES, row.shape[1]))
    return jnp.concatenate([wide[:, k : k + LANES].T for k in range(0, row.shape[1], LANES)], axis=0)


def one_hot(column, width):
    lane = lax.broadcasted_iota(jnp.int32, column.shape, 1)
    return jnp.concatenate(
        [jnp.where(column == lane + k, 1.0, 0.0).astype(BF16) for k in range(0, width, LANES)], axis=1
    )


def spread(rows, head_size):
    lane = lax.broadcasted_iota(jnp.int32, rows.shape, 1) // head_size
    return jnp.concatenate([jnp.where(lane == k, rows, 0) for k in range(LANES // head_size)], axis=0)


def gather(span, row, first_row, all_rows):
    offset = row - first_row
    offset = jnp.where(offset < 0, offset + all_rows, offset)
    offset = jnp.where(offset >= all_rows, offset - all_rows, offset)
    return mm(one_hot(column_of(offset), SPAN), span).astype(BF16)


def self_scores(keys, query, tile, head_size):
    lanes = slice(tile * LANES, (tile + 1) * LANES)
    return mm(spread(keys[:, lanes], head_size), query[:, lanes], NT)


def self_weights(scores, head_size):
    scale = math.log2(math.e) / math.sqrt(head_size)
    heads = LANES // head_size
    count = scores.shape[0] // heads
    return [softmax_down(scores[k * count : (k + 1) * count], scale) for k in range(heads)]


def cross_attention(keys, values, query, head_size):
    scale = math.log2(math.e) / math.sqrt(head_size)
    per_tile = LANES // head_size
    tiles = [slice(k, k + LANES) for k in range(0, query.shape[1], LANES)]
    scores = [mm(spread(keys[:, tile], head_size), query[:, tile], NT) for tile in tiles]
    out = []
    for tile, score in zip(tiles, scores):
        weights = [softmax_down(score[k * PWIN : (k + 1) * PWIN], scale) for k in range(per_tile)]
        out.append(mm(spread(values[:, tile], head_size), jnp.concatenate(weights, axis=0), TN).astype(BF16))
    return jnp.concatenate(out, axis=0)


def span_start(w, rows):
    return lax.axis_index("pix") * rows + w * WIN - HALO


def block(w, size):
    return pl.ds(pl.multiple_of(w * size, size), size)


def pack_rows(parents, slots, packed):
    chunks, height, _ = packed.shape
    count = parents.shape[0] // chunks
    wide = jnp.broadcast_to(slots, (height - count * (parents.shape[1] // LANES), slots.shape[1])).astype(F32)
    for d in range(chunks):
        for c in range(parents.shape[1] // LANES):
            packed[d, c * count : (c + 1) * count] = parents[d * count : (d + 1) * count, c * LANES : (c + 1) * LANES]
        shift = (-d * count) % slots.shape[1]
        turned = pltpu.roll(wide, shift, 1) if shift else wide
        packed[d, height - wide.shape[0] :] = turned[:, :LANES].astype(BF16)


def unpack_rows(arrived, parents, features):
    chunks, height, _ = arrived.shape
    count = parents // chunks
    tiles = features // LANES
    rows = jnp.concatenate(
        [
            jnp.concatenate([arrived[d, c * count : (c + 1) * count] for d in range(chunks)], axis=0)
            for c in range(tiles)
        ],
        axis=1,
    )
    slots = []
    for d in range(chunks):
        begin = d * count % LANES
        part = arrived[d, tiles * count :].astype(F32)
        if begin == 0:
            slots.append(part)
        else:
            lane = lax.broadcasted_iota(jnp.int32, part.shape, 1)
            slots[-1] = jnp.where(lane < begin, slots[-1], pltpu.roll(part, begin, 1))
    return rows, jnp.concatenate(slots, axis=1)[:1].astype(jnp.int32)


def pack_kernel(
    fine, parents, slots, index, gain, parent_gain, first, second, packed, normed, index_v, gains,
    fine_s, parents_s, slots_s, packed_s, sems, *, windows, tight,
):
    rows, features = fine.shape
    odd = lax.rem(lax.axis_index("pix"), 2)
    pieces = [
        (slots, slots_s),
        (parents, parents_s),
        (fine.at[pl.ds(pl.multiple_of((1 - odd) * (rows - HALO), HALO), HALO)], first),
        (fine.at[pl.ds(pl.multiple_of(odd * (rows - HALO), HALO), HALO)], second),
        (gain, gains.at[0]),
        (parent_gain, gains.at[1]),
        (index, index_v),
    ]
    blocks = [slice(w * WIN, (w + 1) * WIN) for w in range(windows)]
    pieces += [(fine.at[here], fine_s.at[here]) for here in blocks]
    pieces += [(packed_s, packed)]
    copies = [pltpu.make_async_copy(src, dst, sems.at[k]) for k, (src, dst) in enumerate(pieces)]
    for copy in copies[:-1]:
        copy.start()
    copies[0].wait()
    copies[1].wait()
    if tight:
        pack_rows(parents_s, slots_s[...], packed_s)
    else:
        packed_s[:, :features] = parents_s[...]
        packed_s[:, features:] = column_of(slots_s[...]).astype(F32).astype(BF16)
    copies[-1].start()
    for copy in copies[2:7]:
        copy.wait()
    for here, copy in zip(blocks, copies[7:]):
        copy.wait()
        normed[here] = rms_rows(fine_s[here], gains[0])
    copies[-1].wait()


def gate_kernel(before, held, passed):
    pass


def self_kernel(
    normed, index, gains, first, second, w_qkv, w_parent, query, early_h, late, wp, w_q, w_kv, early, ends, gathered, keys,
    values_t, sems,
    *, windows, head_size, all_rows,
):
    rows, features = normed.shape
    own = SPAN - HALO
    fetch = [
        pltpu.make_async_copy(w_qkv.at[:, c * features : (c + 1) * features], to, sems.at[c])
        for c, to in enumerate([w_q, w_kv.at[0], w_kv.at[1]])
    ]
    for copy in fetch:
        copy.start()
    odd = lax.rem(lax.axis_index("pix"), 2) == 1
    ends[0, :HALO] = rms_rows(jnp.where(odd, first[...], second[...]), gains[0])
    ends[0, HALO:] = normed[:own]
    ends[1, :own] = normed[rows - own :]
    ends[1, own:] = rms_rows(jnp.where(odd, second[...], first[...]), gains[0])

    def pick(w, span):
        gathered[block(w, WIN)] = gather(span, index[w], span_start(w, rows), all_rows)

    def pick_inner(w, carry):
        pick(w, normed[pl.ds(pl.multiple_of(w * WIN - HALO, HALO), SPAN)])
        return carry

    pick(0, ends[0])
    pick(windows - 1, ends[1])
    lax.fori_loop(1, windows - 1, pick_inner, 0)
    fetch[0].wait()
    query[...] = mm(normed[...], w_q[...]).astype(BF16)
    for copy in fetch[1:]:
        copy.wait()
    keys[...] = mm(gathered[...], w_kv[0]).astype(BF16)
    leave = [
        pltpu.make_async_copy(
            w_parent.at[:, c * features : (c + 1) * features], wp.at[c * features : (c + 1) * features], sems.at[3 + c]
        )
        for c in range(2)
    ]
    for copy in leave:
        copy.start()
    split = early.shape[0]
    tiles = range(features // LANES)

    def scores(w, tile):
        here = slice(w * WIN, (w + 1) * WIN)
        return self_scores(keys[here], query[here], tile, head_size)

    def project_values(begin, end):
        values = mm(gathered[...], w_kv[1][:, begin:end]).astype(BF16)
        for w in range(windows):
            values_t[w, begin:end] = values[w * WIN : (w + 1) * WIN].T

    def apply(w, tile, weights):
        out = early.at[w] if w < split else late.at[w - split]
        for k, weight in enumerate(weights):
            head = slice(tile * LANES + k * head_size, tile * LANES + (k + 1) * head_size)
            out[head] = mm(values_t[w, head], weight).astype(BF16)
        if tile == tiles[-1] and w < split:
            leave.append(pltpu.make_async_copy(out, early_h.at[w], sems.at[5 + w]))
            leave[-1].start()

    pending = [scores(0, tile) for tile in tiles]
    before = []
    for w in range(windows):
        coming, weights = [], []
        for tile in tiles:
            if w + 1 < windows:
                coming.append(scores(w + 1, tile))
            weights.append(self_weights(pending[tile], head_size))
            if w == 0 and tile % 2 == 0:
                project_values(tile * LANES, min(tile + 2, len(tiles)) * LANES)
            if w > 0:
                apply(w - 1, tile, before[tile])
        pending, before = coming, weights
    for tile in tiles:
        apply(windows - 1, tile, before[tile])
    for copy in leave:
        copy.wait()


def cross_kernel(
    query, late, gains, arrived, wp, early_h, fine_h, w_out, out, early, fine, wo, out_s, p_keys, p_values, sems,
    *, windows, head_size, all_rows, tight,
):
    rows, features = fine.shape
    fetch = [
        pltpu.make_async_copy(early_h, early, sems.at[1]),
        pltpu.make_async_copy(w_out, wo, sems.at[2]),
        pltpu.make_async_copy(fine_h, fine, sems.at[3]),
    ]
    for copy in fetch:
        copy.start()
    count = p_keys.shape[0]
    if tight:
        parents, slots = unpack_rows(arrived, count, features)
        place = lax.broadcasted_iota(jnp.int32, (count, count), 0)
        places = jnp.where(place == jnp.broadcast_to(slots, (count, count)), 1.0, 0.0).astype(BF16)
        ordered = mm(places, parents).astype(BF16)
    else:
        places = one_hot(arrived[:, features:].astype(F32).astype(jnp.int32), count)
        ordered = mm(places, arrived[:, :features], TN).astype(BF16)
    normed_parents = rms_rows(ordered, gains[1])
    p_keys[...] = mm(normed_parents, wp[:features]).astype(BF16)
    p_values[...] = mm(normed_parents, wp[features:]).astype(BF16)
    split = early.shape[0]
    rows_of = [slice(w * WIN, (w + 1) * WIN) for w in range(windows)]

    def crossed(w):
        own = slice(w * PWIN, (w + 1) * PWIN)
        return cross_attention(p_keys[own], p_values[own], query[rows_of[w]], head_size)

    ahead = [crossed(w) for w in range(2)]
    for copy in fetch:
        copy.wait()
    for w, here in enumerate(rows_of):
        self_t = early[w] if w < split else late[w - split]
        joined = jnp.concatenate([self_t, ahead.pop(0)], axis=0).T
        branch = mm(joined, wo[...])
        out_s[here] = (fine[here].astype(F32) + branch).astype(BF16)
        pltpu.make_async_copy(out_s.at[here], out.at[here], sems.at[0]).start()
        if w + 2 < windows:
            ahead.append(crossed(w + 2))
    pltpu.make_async_copy(out_s, out, sems.at[0]).wait()


def on_device(
    fine_tokens, parent_tokens, shift_table, parent_slot, fine_gain, parent_gain, w_qkv, w_parent, w_out,
):
    rows, features = fine_tokens.shape
    parents = parent_tokens.shape[0]
    devices = lax.axis_size("pix")
    windows = rows // WIN
    share = parents // devices
    tight = share % 16 == 0 and LANES % share == 0 and features % LANES == 0
    packing = (devices, share * (features // LANES) + 16, LANES) if tight else (parents, features + LANES)
    sizes = dict(windows=windows, head_size=features // HEADS, all_rows=rows * devices)
    params = pltpu.CompilerParams(vmem_limit_bytes=32 * MIB)
    semaphores = pltpu.SemaphoreType.DMA

    def near(*shape, dtype=BF16):
        return pltpu.VMEM(shape, dtype)

    def far(x):
        return pltpu.with_memory_space_constraint(x, pltpu.HBM)

    fine, weights = far(fine_tokens), far(w_qkv)
    first, second, packed, normed, index, gains = pl.pallas_call(
        functools.partial(pack_kernel, windows=windows, tight=tight),
        out_shape=[
            near(HALO, features),
            near(HALO, features),
            pltpu.HBM(packing, BF16),
            near(rows, features),
            near(windows, 1, WIN, dtype=jnp.int32),
            near(2, 1, features, dtype=F32),
        ],
        in_specs=[HBM] * 6,
        out_specs=[VMEM, VMEM, HBM] + [VMEM] * 3,
        scratch_shapes=[
            near(rows, features),
            near(parents, features),
            near(1, parents, dtype=jnp.int32),
            near(*packing),
            semaphores((windows + 8,)),
        ],
        compiler_params=params,
        name="pack",
    )(
        fine, far(parent_tokens), far(parent_slot.reshape(1, parents)), far(shift_table.reshape(windows, 1, WIN)),
        far(fine_gain.reshape(1, features)), far(parent_gain.reshape(1, features)),
    )
    pairs = [(i, i + 1 - 2 * (i % 2)) for i in range(devices)]
    across = [(i, (i - 1 + 2 * (i % 2)) % devices) for i in range(devices)]
    first_in = lax.ppermute(first, "pix", pairs)
    second_in = lax.ppermute(second, "pix", across)
    packed = pl.pallas_call(
        gate_kernel,
        out_shape=pltpu.HBM(packing, BF16),
        in_specs=[VMEM, HBM],
        out_specs=HBM,
        input_output_aliases={1: 0},
        compiler_params=params,
        name="gate",
    )(second, far(packed))
    arrived = lax.all_to_all(packed, "pix", split_axis=0, concat_axis=0, tiled=True)

    split = windows // 2
    query, early, late, wp = pl.pallas_call(
        functools.partial(self_kernel, **sizes),
        out_shape=[
            near(rows, features),
            pltpu.HBM((split, features, WIN), BF16),
            near(windows - split, features, WIN),
            near(2 * features, features),
        ],
        in_specs=[VMEM] * 5 + [HBM] * 2,
        out_specs=[VMEM, HBM, VMEM, VMEM],
        input_output_aliases={0: 3} if rows == 2 * features else {},
        scratch_shapes=[
            near(features, features),
            near(2, features, features),
            near(split, features, WIN),
            near(2, SPAN, features),
            near(rows, features),
            near(rows, features),
            near(windows, features, WIN),
            semaphores((5 + split,)),
        ],
        compiler_params=params,
        cost_estimate=pl.CostEstimate(flops=16 * 10**9, bytes_accessed=4 * 10**6, transcendentals=4 * 10**6),
        name="self",
    )(normed, index, gains, first_in, second_in, weights, far(w_parent))

    return pl.pallas_call(
        functools.partial(cross_kernel, tight=tight, **sizes),
        out_shape=pltpu.HBM((rows, features), BF16),
        in_specs=[VMEM] * 5 + [HBM] * 3,
        out_specs=HBM,
        scratch_shapes=[
            near(split, features, WIN),
            near(rows, features),
            near(2 * features, features),
            near(rows, features),
            near(parents, features),
            near(parents, features),
            semaphores((4,)),
        ],
        compiler_params=params,
        cost_estimate=pl.CostEstimate(flops=5 * 10**9, bytes_accessed=6 * 10**6, transcendentals=10**6),
        name="cross",
    )(query, late, gains, arrived, wp, far(early), fine, far(w_out))


def solution(mesh):
    return jax.shard_map(
        on_device,
        mesh=mesh,
        in_specs=(P(("batch", "pix"), None), P(("batch", "pix"), None), P("pix"), P("pix"), P(), P(), P(), P(), P()),
        out_specs=P(("batch", "pix"), None),
        check_vma=False,
    )
```

```python
import functools
import math

import jax
import jax.numpy as jnp
from jax import lax
from jax.experimental import pallas as pl
from jax.experimental.pallas import tpu as pltpu
from jax.sharding import PartitionSpec as P

HEADS = 16
WIN = 256
HALO = 128
PWIN = 64
LANES = 128
SPAN = WIN + 2 * HALO
F32 = jnp.float32
BF16 = jnp.bfloat16
VMEM = pl.BlockSpec(memory_space=pltpu.VMEM)
HBM = pl.BlockSpec(memory_space=pltpu.HBM)
MIB = 1024 * 1024
NN, NT, TN = ((1,), (0,)), ((1,), (1,)), ((0,), (0,))


def mm(a, b, dims=NN):
    return lax.dot_general(a, b, (dims, ((), ())), preferred_element_type=F32)


def rms_rows(matrix, gain):
    values = matrix.astype(F32)
    factor = lax.rsqrt(jnp.mean(values * values, axis=-1, keepdims=True) + 1e-06)
    return (values * factor * gain).astype(BF16)


def softmax_down(scores, scale):
    powers = jnp.exp2((scores - jnp.max(scores, axis=0, keepdims=True)) * scale)
    return (powers * (1.0 / jnp.sum(powers, axis=0, keepdims=True))).astype(BF16)


def column_of(row):
    wide = jnp.broadcast_to(row, (LANES, row.shape[1]))
    return jnp.concatenate([wide[:, k : k + LANES].T for k in range(0, row.shape[1], LANES)], axis=0)


def one_hot(column, width):
    lane = lax.broadcasted_iota(jnp.int32, column.shape, 1)
    return jnp.concatenate(
        [jnp.where(column == lane + k, 1.0, 0.0).astype(BF16) for k in range(0, width, LANES)], axis=1
    )


def spread(rows, head_size):
    lane = lax.broadcasted_iota(jnp.int32, rows.shape, 1) // head_size
    return jnp.concatenate([jnp.where(lane == k, rows, 0) for k in range(LANES // head_size)], axis=0)


def gather(span, row, first_row, all_rows):
    offset = row - first_row
    offset = jnp.where(offset < 0, offset + all_rows, offset)
    offset = jnp.where(offset >= all_rows, offset - all_rows, offset)
    return mm(one_hot(column_of(offset), SPAN), span).astype(BF16)


def self_scores(keys, query, tile, head_size):
    lanes = slice(tile * LANES, (tile + 1) * LANES)
    return mm(spread(keys[:, lanes], head_size), query[:, lanes], NT)


def self_weights(scores, head_size):
    scale = math.log2(math.e) / math.sqrt(head_size)
    heads = LANES // head_size
    count = scores.shape[0] // heads
    return [softmax_down(scores[k * count : (k + 1) * count], scale) for k in range(heads)]


def cross_attention(keys, values, query, head_size):
    scale = math.log2(math.e) / math.sqrt(head_size)
    per_tile = LANES // head_size
    tiles = [slice(k, k + LANES) for k in range(0, query.shape[1], LANES)]
    scores = [mm(spread(keys[:, tile], head_size), query[:, tile], NT) for tile in tiles]
    out = []
    for tile, score in zip(tiles, scores):
        weights = [softmax_down(score[k * PWIN : (k + 1) * PWIN], scale) for k in range(per_tile)]
        out.append(mm(spread(values[:, tile], head_size), jnp.concatenate(weights, axis=0), TN).astype(BF16))
    return jnp.concatenate(out, axis=0)


def span_start(w, rows):
    return lax.axis_index("pix") * rows + w * WIN - HALO


def block(w, size):
    return pl.ds(pl.multiple_of(w * size, size), size)


def pack_rows(parents, slots, packed, order):
    chunks, height, _ = packed.shape
    count = parents.shape[0] // chunks
    wide = jnp.broadcast_to(slots, (height - count * (parents.shape[1] // LANES), slots.shape[1])).astype(F32)
    for d, owner in enumerate(order):
        own = slice(owner * count, (owner + 1) * count)
        for c in range(parents.shape[1] // LANES):
            packed[d, c * count : (c + 1) * count] = parents[own, c * LANES : (c + 1) * LANES]
        shift = (-owner * count) % slots.shape[1]
        turned = pltpu.roll(wide, shift, 1) if shift else wide
        packed[d, height - wide.shape[0] :] = turned[:, :LANES].astype(BF16)


def unpack_rows(arrived, parents, features):
    chunks, height, _ = arrived.shape
    count = parents // chunks
    tiles = features // LANES
    rows = jnp.concatenate(
        [
            jnp.concatenate([arrived[d, c * count : (c + 1) * count] for d in range(chunks)], axis=0)
            for c in range(tiles)
        ],
        axis=1,
    )
    slots = []
    for d in range(chunks):
        begin = d * count % LANES
        part = arrived[d, tiles * count :].astype(F32)
        if begin == 0:
            slots.append(part)
        else:
            lane = lax.broadcasted_iota(jnp.int32, part.shape, 1)
            slots[-1] = jnp.where(lane < begin, slots[-1], pltpu.roll(part, begin, 1))
    return rows, jnp.concatenate(slots, axis=1)[:1].astype(jnp.int32)


def pack_kernel(
    fine, parents, slots, index, gain, parent_gain, first, second, packed, normed, index_v, gains,
    fine_s, parents_s, slots_s, packed_s, sems, *, windows, order,
):
    rows, features = fine.shape
    odd = lax.rem(lax.axis_index("pix"), 2)
    pieces = [
        (slots, slots_s),
        (parents, parents_s),
        (fine.at[pl.ds(pl.multiple_of((1 - odd) * (rows - HALO), HALO), HALO)], first),
        (fine.at[pl.ds(pl.multiple_of(odd * (rows - HALO), HALO), HALO)], second),
        (gain, gains.at[0]),
        (parent_gain, gains.at[1]),
        (index, index_v),
    ]
    blocks = [slice(w * WIN, (w + 1) * WIN) for w in range(windows)]
    pieces += [(fine.at[here], fine_s.at[here]) for here in blocks]
    pieces += [(packed_s, packed)]
    copies = [pltpu.make_async_copy(src, dst, sems.at[k]) for k, (src, dst) in enumerate(pieces)]
    for copy in copies[:-1]:
        copy.start()
    copies[0].wait()
    copies[1].wait()
    if order:
        pack_rows(parents_s, slots_s[...], packed_s, order)
    else:
        packed_s[:, :features] = parents_s[...]
        packed_s[:, features:] = column_of(slots_s[...]).astype(F32).astype(BF16)
    copies[-1].start()
    for copy in copies[2:7]:
        copy.wait()
    for here, copy in zip(blocks, copies[7:]):
        copy.wait()
        normed[here] = rms_rows(fine_s[here], gains[0])
    copies[-1].wait()


def gate_kernel(before, held, passed):
    pass


def self_kernel(
    normed, index, gains, first, second, w_qkv, w_parent, query, early_h, late, wp, w_q, w_kv, early, ends, gathered, keys,
    values_t, sems,
    *, windows, head_size, all_rows,
):
    rows, features = normed.shape
    own = SPAN - HALO
    fetch = [
        pltpu.make_async_copy(w_qkv.at[:, c * features : (c + 1) * features], to, sems.at[c])
        for c, to in enumerate([w_q, w_kv.at[0], w_kv.at[1]])
    ]
    for copy in fetch:
        copy.start()
    odd = lax.rem(lax.axis_index("pix"), 2) == 1
    ends[0, :HALO] = rms_rows(jnp.where(odd, first[...], second[...]), gains[0])
    ends[0, HALO:] = normed[:own]
    ends[1, :own] = normed[rows - own :]
    ends[1, own:] = rms_rows(jnp.where(odd, second[...], first[...]), gains[0])

    def pick(w, span):
        gathered[block(w, WIN)] = gather(span, index[w], span_start(w, rows), all_rows)

    def pick_inner(w, carry):
        pick(w, normed[pl.ds(pl.multiple_of(w * WIN - HALO, HALO), SPAN)])
        return carry

    pick(0, ends[0])
    pick(windows - 1, ends[1])
    lax.fori_loop(1, windows - 1, pick_inner, 0)
    fetch[0].wait()
    query[...] = mm(normed[...], w_q[...]).astype(BF16)
    for copy in fetch[1:]:
        copy.wait()
    keys[...] = mm(gathered[...], w_kv[0]).astype(BF16)
    leave = [
        pltpu.make_async_copy(
            w_parent.at[:, c * features : (c + 1) * features], wp.at[c * features : (c + 1) * features], sems.at[3 + c]
        )
        for c in range(2)
    ]
    for copy in leave:
        copy.start()
    split = early.shape[0]
    tiles = range(features // LANES)

    def scores(w, tile):
        here = slice(w * WIN, (w + 1) * WIN)
        return self_scores(keys[here], query[here], tile, head_size)

    def project_values(begin, end):
        values = mm(gathered[...], w_kv[1][:, begin:end]).astype(BF16)
        for w in range(windows):
            values_t[w, begin:end] = values[w * WIN : (w + 1) * WIN].T

    def apply(w, tile, weights):
        out = early.at[w] if w < split else late.at[w - split]
        for k, weight in enumerate(weights):
            head = slice(tile * LANES + k * head_size, tile * LANES + (k + 1) * head_size)
            out[head] = mm(values_t[w, head], weight).astype(BF16)
        if tile == tiles[-1] and w < split:
            leave.append(pltpu.make_async_copy(out, early_h.at[w], sems.at[5 + w]))
            leave[-1].start()

    pending = [scores(0, tile) for tile in tiles]
    before = []
    for w in range(windows):
        coming, weights = [], []
        for tile in tiles:
            if w + 1 < windows:
                coming.append(scores(w + 1, tile))
            weights.append(self_weights(pending[tile], head_size))
            if w == 0 and tile % 2 == 0:
                project_values(tile * LANES, min(tile + 2, len(tiles)) * LANES)
            if w > 0:
                apply(w - 1, tile, before[tile])
        pending, before = coming, weights
    for tile in tiles:
        apply(windows - 1, tile, before[tile])
    for copy in leave:
        copy.wait()


def cross_kernel(
    query, late, gains, arrived, wp, early_h, fine_h, w_out, out, early, fine, wo, out_s, p_keys, p_values, sems,
    *, windows, head_size, all_rows, tight,
):
    rows, features = fine.shape
    fetch = [
        pltpu.make_async_copy(early_h, early, sems.at[1]),
        pltpu.make_async_copy(w_out, wo, sems.at[2]),
        pltpu.make_async_copy(fine_h, fine, sems.at[3]),
    ]
    for copy in fetch:
        copy.start()
    count = p_keys.shape[0]
    if tight:
        parents, slots = unpack_rows(arrived, count, features)
        place = lax.broadcasted_iota(jnp.int32, (count, count), 0)
        places = jnp.where(place == jnp.broadcast_to(slots, (count, count)), 1.0, 0.0).astype(BF16)
        ordered = mm(places, parents).astype(BF16)
    else:
        places = one_hot(arrived[:, features:].astype(F32).astype(jnp.int32), count)
        ordered = mm(places, arrived[:, :features], TN).astype(BF16)
    normed_parents = rms_rows(ordered, gains[1])
    p_keys[...] = mm(normed_parents, wp[:features]).astype(BF16)
    p_values[...] = mm(normed_parents, wp[features:]).astype(BF16)
    split = early.shape[0]
    rows_of = [slice(w * WIN, (w + 1) * WIN) for w in range(windows)]

    def crossed(w):
        own = slice(w * PWIN, (w + 1) * PWIN)
        return cross_attention(p_keys[own], p_values[own], query[rows_of[w]], head_size)

    ahead = [crossed(w) for w in range(2)]
    for copy in fetch:
        copy.wait()
    for w, here in enumerate(rows_of):
        self_t = early[w] if w < split else late[w - split]
        joined = jnp.concatenate([self_t, ahead.pop(0)], axis=0).T
        branch = mm(joined, wo[...])
        out_s[here] = (fine[here].astype(F32) + branch).astype(BF16)
        pltpu.make_async_copy(out_s.at[here], out.at[here], sems.at[0]).start()
        if w + 2 < windows:
            ahead.append(crossed(w + 2))
    pltpu.make_async_copy(out_s, out, sems.at[0]).wait()


def on_device(
    fine_tokens, parent_tokens, shift_table, parent_slot, fine_gain, parent_gain, w_qkv, w_parent, w_out,
):
    rows, features = fine_tokens.shape
    parents = parent_tokens.shape[0]
    devices = lax.axis_size("pix")
    windows = rows // WIN
    share = parents // devices
    tight = share % 16 == 0 and LANES % share == 0 and features % LANES == 0
    packing = (devices, share * (features // LANES) + 16, LANES) if tight else (parents, features + LANES)
    order = tuple((d + devices // 4) % devices for d in range(devices)) if tight else None
    sizes = dict(windows=windows, head_size=features // HEADS, all_rows=rows * devices)
    params = pltpu.CompilerParams(vmem_limit_bytes=32 * MIB)
    semaphores = pltpu.SemaphoreType.DMA

    def near(*shape, dtype=BF16):
        return pltpu.VMEM(shape, dtype)

    def far(x):
        return pltpu.with_memory_space_constraint(x, pltpu.HBM)

    fine, weights = far(fine_tokens), far(w_qkv)
    first, second, packed, normed, index, gains = pl.pallas_call(
        functools.partial(pack_kernel, windows=windows, order=order),
        out_shape=[
            near(HALO, features),
            near(HALO, features),
            pltpu.HBM(packing, BF16),
            near(rows, features),
            near(windows, 1, WIN, dtype=jnp.int32),
            near(2, 1, features, dtype=F32),
        ],
        in_specs=[HBM] * 6,
        out_specs=[VMEM, VMEM, HBM] + [VMEM] * 3,
        scratch_shapes=[
            near(rows, features),
            near(parents, features),
            near(1, parents, dtype=jnp.int32),
            near(*packing),
            semaphores((windows + 8,)),
        ],
        compiler_params=params,
        name="pack",
    )(
        fine, far(parent_tokens), far(parent_slot.reshape(1, parents)), far(shift_table.reshape(windows, 1, WIN)),
        far(fine_gain.reshape(1, features)), far(parent_gain.reshape(1, features)),
    )
    pairs = [(i, i + 1 - 2 * (i % 2)) for i in range(devices)]
    across = [(i, (i - 1 + 2 * (i % 2)) % devices) for i in range(devices)]
    first_in = lax.ppermute(first, "pix", pairs)
    second_in = lax.ppermute(second, "pix", across)
    packed = pl.pallas_call(
        gate_kernel,
        out_shape=pltpu.HBM(packing, BF16),
        in_specs=[VMEM, HBM],
        out_specs=HBM,
        input_output_aliases={1: 0},
        compiler_params=params,
        name="gate",
    )(second, far(packed))
    groups = [list(order)] if tight else None
    arrived = lax.all_to_all(packed, "pix", split_axis=0, concat_axis=0, tiled=True, axis_index_groups=groups)

    split = windows // 2
    query, early, late, wp = pl.pallas_call(
        functools.partial(self_kernel, **sizes),
        out_shape=[
            near(rows, features),
            pltpu.HBM((split, features, WIN), BF16),
            near(windows - split, features, WIN),
            near(2 * features, features),
        ],
        in_specs=[VMEM] * 5 + [HBM] * 2,
        out_specs=[VMEM, HBM, VMEM, VMEM],
        input_output_aliases={0: 3} if rows == 2 * features else {},
        scratch_shapes=[
            near(features, features),
            near(2, features, features),
            near(split, features, WIN),
            near(2, SPAN, features),
            near(rows, features),
            near(rows, features),
            near(windows, features, WIN),
            semaphores((5 + split,)),
        ],
        compiler_params=params,
        cost_estimate=pl.CostEstimate(flops=16 * 10**9, bytes_accessed=4 * 10**6, transcendentals=4 * 10**6),
        name="self",
    )(normed, index, gains, first_in, second_in, weights, far(w_parent))

    return pl.pallas_call(
        functools.partial(cross_kernel, tight=tight, **sizes),
        out_shape=pltpu.HBM((rows, features), BF16),
        in_specs=[VMEM] * 5 + [HBM] * 3,
        out_specs=HBM,
        scratch_shapes=[
            near(split, features, WIN),
            near(rows, features),
            near(2 * features, features),
            near(rows, features),
            near(parents, features),
            near(parents, features),
            semaphores((4,)),
        ],
        compiler_params=params,
        cost_estimate=pl.CostEstimate(flops=5 * 10**9, bytes_accessed=6 * 10**6, transcendentals=10**6),
        name="cross",
    )(query, late, gains, arrived, wp, far(early), fine, far(w_out))


def solution(mesh):
    return jax.shard_map(
        on_device,
        mesh=mesh,
        in_specs=(P(("batch", "pix"), None), P(("batch", "pix"), None), P("pix"), P("pix"), P(), P(), P(), P(), P()),
        out_specs=P(("batch", "pix"), None),
        check_vma=False,
    )
```

```python
import functools
import math

import jax
import jax.numpy as jnp
from jax import lax
from jax.experimental import pallas as pl
from jax.experimental.pallas import tpu as pltpu
from jax.sharding import PartitionSpec as P

HEADS = 16
WIN = 256
HALO = 128
PWIN = 64
LANES = 128
SPAN = WIN + 2 * HALO
F32 = jnp.float32
BF16 = jnp.bfloat16
VMEM = pl.BlockSpec(memory_space=pltpu.VMEM)
HBM = pl.BlockSpec(memory_space=pltpu.HBM)
MIB = 1024 * 1024
NN, NT, TN = ((1,), (0,)), ((1,), (1,)), ((0,), (0,))


def mm(a, b, dims=NN):
    return lax.dot_general(a, b, (dims, ((), ())), preferred_element_type=F32)


def rms_rows(matrix, gain):
    values = matrix.astype(F32)
    factor = lax.rsqrt(jnp.mean(values * values, axis=-1, keepdims=True) + 1e-06)
    return (values * factor * gain).astype(BF16)


def softmax_down(scores, scale):
    powers = jnp.exp2((scores - jnp.max(scores, axis=0, keepdims=True)) * scale)
    return (powers * (1.0 / jnp.sum(powers, axis=0, keepdims=True))).astype(BF16)


def column_of(row):
    wide = jnp.broadcast_to(row, (LANES, row.shape[1]))
    return jnp.concatenate([wide[:, k : k + LANES].T for k in range(0, row.shape[1], LANES)], axis=0)


def one_hot(column, width):
    lane = lax.broadcasted_iota(jnp.int32, column.shape, 1)
    return jnp.concatenate(
        [jnp.where(column == lane + k, 1.0, 0.0).astype(BF16) for k in range(0, width, LANES)], axis=1
    )


def spread(rows, head_size):
    lane = lax.broadcasted_iota(jnp.int32, rows.shape, 1) // head_size
    return jnp.concatenate([jnp.where(lane == k, rows, 0) for k in range(LANES // head_size)], axis=0)


def gather(span, row, first_row, all_rows):
    offset = row - first_row
    offset = jnp.where(offset < 0, offset + all_rows, offset)
    offset = jnp.where(offset >= all_rows, offset - all_rows, offset)
    return mm(one_hot(column_of(offset), SPAN), span).astype(BF16)


def self_scores(keys, query, tile, head_size):
    lanes = slice(tile * LANES, (tile + 1) * LANES)
    return mm(spread(keys[:, lanes], head_size), query[:, lanes], NT)


def self_weights(scores, head_size):
    scale = math.log2(math.e) / math.sqrt(head_size)
    heads = LANES // head_size
    count = scores.shape[0] // heads
    return [softmax_down(scores[k * count : (k + 1) * count], scale) for k in range(heads)]


def cross_attention(keys, values, query, head_size):
    scale = math.log2(math.e) / math.sqrt(head_size)
    per_tile = LANES // head_size
    tiles = [slice(k, k + LANES) for k in range(0, query.shape[1], LANES)]
    scores = [mm(spread(keys[:, tile], head_size), query[:, tile], NT) for tile in tiles]
    out = []
    for tile, score in zip(tiles, scores):
        weights = [softmax_down(score[k * PWIN : (k + 1) * PWIN], scale) for k in range(per_tile)]
        out.append(mm(spread(values[:, tile], head_size), jnp.concatenate(weights, axis=0), TN).astype(BF16))
    return jnp.concatenate(out, axis=0)


def span_start(w, rows):
    return lax.axis_index("pix") * rows + w * WIN - HALO


def block(w, size):
    return pl.ds(pl.multiple_of(w * size, size), size)


def pack_rows(parents, slots, packed, order):
    chunks, height, _ = packed.shape
    count = parents.shape[0] // chunks
    wide = jnp.broadcast_to(slots, (height - count * (parents.shape[1] // LANES), slots.shape[1])).astype(F32)
    for d, owner in enumerate(order):
        own = slice(owner * count, (owner + 1) * count)
        for c in range(parents.shape[1] // LANES):
            packed[d, c * count : (c + 1) * count] = parents[own, c * LANES : (c + 1) * LANES]
        shift = (-owner * count) % slots.shape[1]
        turned = pltpu.roll(wide, shift, 1) if shift else wide
        packed[d, height - wide.shape[0] :] = turned[:, :LANES].astype(BF16)


def unpack_rows(arrived, parents, features):
    chunks, height, _ = arrived.shape
    count = parents // chunks
    tiles = features // LANES
    rows = jnp.concatenate(
        [
            jnp.concatenate([arrived[d, c * count : (c + 1) * count] for d in range(chunks)], axis=0)
            for c in range(tiles)
        ],
        axis=1,
    )
    slots = []
    for d in range(chunks):
        begin = d * count % LANES
        part = arrived[d, tiles * count :].astype(F32)
        if begin == 0:
            slots.append(part)
        else:
            lane = lax.broadcasted_iota(jnp.int32, part.shape, 1)
            slots[-1] = jnp.where(lane < begin, slots[-1], pltpu.roll(part, begin, 1))
    return rows, jnp.concatenate(slots, axis=1)[:1].astype(jnp.int32)


def pack_kernel(
    fine, parents, slots, index, gain, parent_gain, first, second, packed, fine_v, index_v, gains, parents_s, slots_s, sems,
    *, order,
):
    rows, features = fine.shape
    odd = lax.rem(lax.axis_index("pix"), 2)
    pieces = [
        (slots, slots_s),
        (parents, parents_s),
        (fine.at[pl.ds(pl.multiple_of((1 - odd) * (rows - HALO), HALO), HALO)], first),
        (fine.at[pl.ds(pl.multiple_of(odd * (rows - HALO), HALO), HALO)], second),
        (gain, gains.at[0]),
        (parent_gain, gains.at[1]),
        (index, index_v),
        (fine, fine_v),
    ]
    copies = [pltpu.make_async_copy(src, dst, sems.at[k]) for k, (src, dst) in enumerate(pieces)]
    for copy in copies:
        copy.start()
    copies[0].wait()
    copies[1].wait()
    if order:
        pack_rows(parents_s, slots_s[...], packed, order)
    else:
        packed[:, :features] = parents_s[...]
        packed[:, features:] = column_of(slots_s[...]).astype(F32).astype(BF16)
    for copy in copies[2:]:
        copy.wait()


def norm_kernel(before, packed, fine, gains, passed, normed, sem):
    copy = pltpu.make_async_copy(packed, passed, sem)
    copy.start()
    for start in range(0, fine.shape[0], WIN):
        normed[start : start + WIN] = rms_rows(fine[start : start + WIN], gains[0])
    copy.wait()


def self_kernel(
    normed, index, gains, first, second, w_qkv, w_parent, query, early_h, late, wp, w_q, w_kv, early, ends, gathered, keys,
    values_t, sems,
    *, windows, head_size, all_rows,
):
    rows, features = normed.shape
    own = SPAN - HALO
    fetch = [
        pltpu.make_async_copy(w_qkv.at[:, c * features : (c + 1) * features], to, sems.at[c])
        for c, to in enumerate([w_q, w_kv.at[0], w_kv.at[1]])
    ]
    for copy in fetch:
        copy.start()
    odd = lax.rem(lax.axis_index("pix"), 2) == 1
    ends[0, :HALO] = rms_rows(jnp.where(odd, first[...], second[...]), gains[0])
    ends[0, HALO:] = normed[:own]
    ends[1, :own] = normed[rows - own :]
    ends[1, own:] = rms_rows(jnp.where(odd, second[...], first[...]), gains[0])

    def pick(w, span):
        gathered[block(w, WIN)] = gather(span, index[w], span_start(w, rows), all_rows)

    def pick_inner(w, carry):
        pick(w, normed[pl.ds(pl.multiple_of(w * WIN - HALO, HALO), SPAN)])
        return carry

    pick(0, ends[0])
    pick(windows - 1, ends[1])
    lax.fori_loop(1, windows - 1, pick_inner, 0)
    fetch[0].wait()
    query[...] = mm(normed[...], w_q[...]).astype(BF16)
    for copy in fetch[1:]:
        copy.wait()
    keys[...] = mm(gathered[...], w_kv[0]).astype(BF16)
    leave = [
        pltpu.make_async_copy(
            w_parent.at[:, c * features : (c + 1) * features], wp.at[c * features : (c + 1) * features], sems.at[3 + c]
        )
        for c in range(2)
    ]
    for copy in leave:
        copy.start()
    split = early.shape[0]
    tiles = range(features // LANES)

    def scores(w, tile):
        here = slice(w * WIN, (w + 1) * WIN)
        return self_scores(keys[here], query[here], tile, head_size)

    def project_values(begin, end):
        values = mm(gathered[...], w_kv[1][:, begin:end]).astype(BF16)
        for w in range(windows):
            values_t[w, begin:end] = values[w * WIN : (w + 1) * WIN].T

    def apply(w, tile, weights):
        out = early.at[w] if w < split else late.at[w - split]
        for k, weight in enumerate(weights):
            head = slice(tile * LANES + k * head_size, tile * LANES + (k + 1) * head_size)
            out[head] = mm(values_t[w, head], weight).astype(BF16)
        if tile == tiles[-1] and w < split:
            leave.append(pltpu.make_async_copy(out, early_h.at[w], sems.at[5 + w]))
            leave[-1].start()

    pending = [scores(0, tile) for tile in tiles]
    before = []
    for w in range(windows):
        coming, weights = [], []
        for tile in tiles:
            if w + 1 < windows:
                coming.append(scores(w + 1, tile))
            weights.append(self_weights(pending[tile], head_size))
            if w == 0 and tile % 2 == 0:
                project_values(tile * LANES, min(tile + 2, len(tiles)) * LANES)
            if w > 0:
                apply(w - 1, tile, before[tile])
        pending, before = coming, weights
    for tile in tiles:
        apply(windows - 1, tile, before[tile])
    for copy in leave:
        copy.wait()


def cross_kernel(
    query, late, gains, arrived, wp, early_h, fine_h, w_out, out, early, fine, wo, out_s, p_keys, p_values, sems,
    *, windows, head_size, all_rows, tight,
):
    rows, features = fine.shape
    fetch = [
        pltpu.make_async_copy(early_h, early, sems.at[1]),
        pltpu.make_async_copy(w_out, wo, sems.at[2]),
        pltpu.make_async_copy(fine_h, fine, sems.at[3]),
    ]
    for copy in fetch:
        copy.start()
    count = p_keys.shape[0]
    if tight:
        parents, slots = unpack_rows(arrived, count, features)
        place = lax.broadcasted_iota(jnp.int32, (count, count), 0)
        places = jnp.where(place == jnp.broadcast_to(slots, (count, count)), 1.0, 0.0).astype(BF16)
        ordered = mm(places, parents).astype(BF16)
    else:
        places = one_hot(arrived[:, features:].astype(F32).astype(jnp.int32), count)
        ordered = mm(places, arrived[:, :features], TN).astype(BF16)
    normed_parents = rms_rows(ordered, gains[1])
    p_keys[...] = mm(normed_parents, wp[:features]).astype(BF16)
    p_values[...] = mm(normed_parents, wp[features:]).astype(BF16)
    split = early.shape[0]
    rows_of = [slice(w * WIN, (w + 1) * WIN) for w in range(windows)]

    def crossed(w):
        own = slice(w * PWIN, (w + 1) * PWIN)
        return cross_attention(p_keys[own], p_values[own], query[rows_of[w]], head_size)

    ahead = [crossed(w) for w in range(2)]
    for copy in fetch:
        copy.wait()
    for w, here in enumerate(rows_of):
        self_t = early[w] if w < split else late[w - split]
        joined = jnp.concatenate([self_t, ahead.pop(0)], axis=0).T
        branch = mm(joined, wo[...])
        out_s[here] = (fine[here].astype(F32) + branch).astype(BF16)
        pltpu.make_async_copy(out_s.at[here], out.at[here], sems.at[0]).start()
        if w + 2 < windows:
            ahead.append(crossed(w + 2))
    pltpu.make_async_copy(out_s, out, sems.at[0]).wait()


def on_device(
    fine_tokens, parent_tokens, shift_table, parent_slot, fine_gain, parent_gain, w_qkv, w_parent, w_out,
):
    rows, features = fine_tokens.shape
    parents = parent_tokens.shape[0]
    devices = lax.axis_size("pix")
    windows = rows // WIN
    share = parents // devices
    tight = share % 16 == 0 and LANES % share == 0 and features % LANES == 0
    packing = (devices, share * (features // LANES) + 16, LANES) if tight else (parents, features + LANES)
    order = tuple((d + devices // 4) % devices for d in range(devices)) if tight else None
    sizes = dict(windows=windows, head_size=features // HEADS, all_rows=rows * devices)
    params = pltpu.CompilerParams(vmem_limit_bytes=32 * MIB)
    semaphores = pltpu.SemaphoreType.DMA

    def near(*shape, dtype=BF16):
        return pltpu.VMEM(shape, dtype)

    def far(x):
        return pltpu.with_memory_space_constraint(x, pltpu.HBM)

    fine, weights = far(fine_tokens), far(w_qkv)
    first, second, packed, fine_v, index, gains = pl.pallas_call(
        functools.partial(pack_kernel, order=order),
        out_shape=[
            near(HALO, features),
            near(HALO, features),
            near(*packing),
            near(rows, features),
            near(windows, 1, WIN, dtype=jnp.int32),
            near(2, 1, features, dtype=F32),
        ],
        in_specs=[HBM] * 6,
        out_specs=[VMEM] * 6,
        scratch_shapes=[
            near(parents, features),
            near(1, parents, dtype=jnp.int32),
            semaphores((8,)),
        ],
        compiler_params=params,
        name="pack",
    )(
        fine, far(parent_tokens), far(parent_slot.reshape(1, parents)), far(shift_table.reshape(windows, 1, WIN)),
        far(fine_gain.reshape(1, features)), far(parent_gain.reshape(1, features)),
    )
    pairs = [(i, i + 1 - 2 * (i % 2)) for i in range(devices)]
    across = [(i, (i - 1 + 2 * (i % 2)) % devices) for i in range(devices)]
    first_in = lax.ppermute(first, "pix", pairs)
    second_in = lax.ppermute(second, "pix", across)
    packed, normed = pl.pallas_call(
        norm_kernel,
        out_shape=[pltpu.HBM(packing, BF16), near(rows, features)],
        in_specs=[VMEM] * 4,
        out_specs=[HBM, VMEM],
        input_output_aliases={2: 1},
        scratch_shapes=[semaphores],
        compiler_params=params,
        name="norm",
    )(second, packed, fine_v, gains)
    groups = [list(order)] if tight else None
    arrived = lax.all_to_all(packed, "pix", split_axis=0, concat_axis=0, tiled=True, axis_index_groups=groups)

    split = windows // 2
    query, early, late, wp = pl.pallas_call(
        functools.partial(self_kernel, **sizes),
        out_shape=[
            near(rows, features),
            pltpu.HBM((split, features, WIN), BF16),
            near(windows - split, features, WIN),
            near(2 * features, features),
        ],
        in_specs=[VMEM] * 5 + [HBM] * 2,
        out_specs=[VMEM, HBM, VMEM, VMEM],
        input_output_aliases={0: 3} if rows == 2 * features else {},
        scratch_shapes=[
            near(features, features),
            near(2, features, features),
            near(split, features, WIN),
            near(2, SPAN, features),
            near(rows, features),
            near(rows, features),
            near(windows, features, WIN),
            semaphores((5 + split,)),
        ],
        compiler_params=params,
        cost_estimate=pl.CostEstimate(flops=16 * 10**9, bytes_accessed=4 * 10**6, transcendentals=4 * 10**6),
        name="self",
    )(normed, index, gains, first_in, second_in, weights, far(w_parent))

    return pl.pallas_call(
        functools.partial(cross_kernel, tight=tight, **sizes),
        out_shape=pltpu.HBM((rows, features), BF16),
        in_specs=[VMEM] * 5 + [HBM] * 3,
        out_specs=HBM,
        scratch_shapes=[
            near(split, features, WIN),
            near(rows, features),
            near(2 * features, features),
            near(rows, features),
            near(parents, features),
            near(parents, features),
            semaphores((4,)),
        ],
        compiler_params=params,
        cost_estimate=pl.CostEstimate(flops=5 * 10**9, bytes_accessed=6 * 10**6, transcendentals=10**6),
        name="cross",
    )(query, late, gains, arrived, wp, far(early), fine, far(w_out))


def solution(mesh):
    return jax.shard_map(
        on_device,
        mesh=mesh,
        in_specs=(P(("batch", "pix"), None), P(("batch", "pix"), None), P("pix"), P("pix"), P(), P(), P(), P(), P()),
        out_specs=P(("batch", "pix"), None),
        check_vma=False,
    )
```

```python
import functools
import math

import jax
import jax.numpy as jnp
from jax import lax
from jax.experimental import pallas as pl
from jax.experimental.pallas import tpu as pltpu
from jax.sharding import PartitionSpec as P

HEADS = 16
WIN = 256
HALO = 128
PWIN = 64
LANES = 128
SPAN = WIN + 2 * HALO
F32 = jnp.float32
BF16 = jnp.bfloat16
VMEM = pl.BlockSpec(memory_space=pltpu.VMEM)
HBM = pl.BlockSpec(memory_space=pltpu.HBM)
MIB = 1024 * 1024
NN, NT, TN = ((1,), (0,)), ((1,), (1,)), ((0,), (0,))


def mm(a, b, dims=NN):
    return lax.dot_general(a, b, (dims, ((), ())), preferred_element_type=F32)


def rms_rows(matrix, gain):
    values = matrix.astype(F32)
    factor = lax.rsqrt(jnp.mean(values * values, axis=-1, keepdims=True) + 1e-06)
    return (values * factor * gain).astype(BF16)


def softmax_down(scores, scale):
    powers = jnp.exp2((scores - jnp.max(scores, axis=0, keepdims=True)) * scale)
    return (powers * (1.0 / jnp.sum(powers, axis=0, keepdims=True))).astype(BF16)


def column_of(row):
    wide = jnp.broadcast_to(row, (LANES, row.shape[1]))
    return jnp.concatenate([wide[:, k : k + LANES].T for k in range(0, row.shape[1], LANES)], axis=0)


def one_hot(column, width):
    lane = lax.broadcasted_iota(jnp.int32, column.shape, 1)
    return jnp.concatenate(
        [jnp.where(column == lane + k, 1.0, 0.0).astype(BF16) for k in range(0, width, LANES)], axis=1
    )


def spread(rows, head_size):
    lane = lax.broadcasted_iota(jnp.int32, rows.shape, 1) // head_size
    return jnp.concatenate([jnp.where(lane == k, rows, 0) for k in range(LANES // head_size)], axis=0)


def gather(span, row, first_row, all_rows):
    offset = row - first_row
    offset = jnp.where(offset < 0, offset + all_rows, offset)
    offset = jnp.where(offset >= all_rows, offset - all_rows, offset)
    return mm(one_hot(column_of(offset), SPAN), span).astype(BF16)


def self_scores(keys, query, tile, head_size):
    lanes = slice(tile * LANES, (tile + 1) * LANES)
    return mm(spread(keys[:, lanes], head_size), query[:, lanes], NT)


def self_weights(scores, head_size):
    scale = math.log2(math.e) / math.sqrt(head_size)
    heads = LANES // head_size
    count = scores.shape[0] // heads
    return [softmax_down(scores[k * count : (k + 1) * count], scale) for k in range(heads)]


def cross_attention(keys, values, query, head_size):
    scale = math.log2(math.e) / math.sqrt(head_size)
    per_tile = LANES // head_size
    tiles = [slice(k, k + LANES) for k in range(0, query.shape[1], LANES)]
    scores = [mm(spread(keys[:, tile], head_size), query[:, tile], NT) for tile in tiles]
    out = []
    for tile, score in zip(tiles, scores):
        weights = [softmax_down(score[k * PWIN : (k + 1) * PWIN], scale) for k in range(per_tile)]
        out.append(mm(spread(values[:, tile], head_size), jnp.concatenate(weights, axis=0), TN).astype(BF16))
    return jnp.concatenate(out, axis=0)


def span_start(w, rows):
    return lax.axis_index("pix") * rows + w * WIN - HALO


def block(w, size):
    return pl.ds(pl.multiple_of(w * size, size), size)


def pack_rows(parents, slots, packed, order):
    chunks, height, _ = packed.shape
    count = parents.shape[0] // chunks
    wide = jnp.broadcast_to(slots, (height - count * (parents.shape[1] // LANES), slots.shape[1])).astype(F32)
    for d, owner in enumerate(order):
        own = slice(owner * count, (owner + 1) * count)
        for c in range(parents.shape[1] // LANES):
            packed[d, c * count : (c + 1) * count] = parents[own, c * LANES : (c + 1) * LANES]
        shift = (-owner * count) % slots.shape[1]
        turned = pltpu.roll(wide, shift, 1) if shift else wide
        packed[d, height - wide.shape[0] :] = turned[:, :LANES].astype(BF16)


def unpack_rows(arrived, parents, features):
    chunks, height, _ = arrived.shape
    count = parents // chunks
    tiles = features // LANES
    rows = jnp.concatenate(
        [
            jnp.concatenate([arrived[d, c * count : (c + 1) * count] for d in range(chunks)], axis=0)
            for c in range(tiles)
        ],
        axis=1,
    )
    slots = []
    for d in range(chunks):
        begin = d * count % LANES
        part = arrived[d, tiles * count :].astype(F32)
        if begin == 0:
            slots.append(part)
        else:
            lane = lax.broadcasted_iota(jnp.int32, part.shape, 1)
            slots[-1] = jnp.where(lane < begin, slots[-1], pltpu.roll(part, begin, 1))
    return rows, jnp.concatenate(slots, axis=1)[:1].astype(jnp.int32)


def pack_kernel(
    fine, parents, slots, index, gain, parent_gain, first, second, packed, fine_v, index_v, gains, parents_s, slots_s, sems,
    *, order,
):
    rows, features = fine.shape
    odd = lax.rem(lax.axis_index("pix"), 2)
    pieces = [
        (slots, slots_s),
        (parents, parents_s),
        (fine.at[pl.ds(pl.multiple_of((1 - odd) * (rows - HALO), HALO), HALO)], first),
        (fine.at[pl.ds(pl.multiple_of(odd * (rows - HALO), HALO), HALO)], second),
        (gain, gains.at[0]),
        (parent_gain, gains.at[1]),
        (index, index_v),
        (fine, fine_v),
    ]
    copies = [pltpu.make_async_copy(src, dst, sems.at[k]) for k, (src, dst) in enumerate(pieces)]
    for copy in copies:
        copy.start()
    copies[0].wait()
    copies[1].wait()
    if order:
        pack_rows(parents_s, slots_s[...], packed, order)
    else:
        packed[:, :features] = parents_s[...]
        packed[:, features:] = column_of(slots_s[...]).astype(F32).astype(BF16)
    for copy in copies[2:]:
        copy.wait()


def norm_kernel(before, packed, fine, gains, passed, normed, sem):
    copy = pltpu.make_async_copy(packed, passed, sem)
    copy.start()
    for start in range(0, fine.shape[0], WIN):
        normed[start : start + WIN] = rms_rows(fine[start : start + WIN], gains[0])
    copy.wait()


def self_kernel(
    normed, index, gains, first, second, w_qkv, w_parent, query, early_h, late, wp, w_q, w_kv, early, ends, gathered, keys,
    values_t, sems,
    *, windows, head_size, all_rows,
):
    rows, features = normed.shape
    own = SPAN - HALO
    fetch = [
        pltpu.make_async_copy(w_qkv.at[:, c * features : (c + 1) * features], to, sems.at[c])
        for c, to in enumerate([w_q, w_kv.at[0], w_kv.at[1]])
    ]
    for copy in fetch:
        copy.start()
    odd = lax.rem(lax.axis_index("pix"), 2) == 1
    ends[0, :HALO] = rms_rows(jnp.where(odd, first[...], second[...]), gains[0])
    ends[0, HALO:] = normed[:own]
    ends[1, :own] = normed[rows - own :]
    ends[1, own:] = rms_rows(jnp.where(odd, second[...], first[...]), gains[0])

    def pick(w, span):
        gathered[block(w, WIN)] = gather(span, index[w], span_start(w, rows), all_rows)

    def pick_inner(w, carry):
        pick(w, normed[pl.ds(pl.multiple_of(w * WIN - HALO, HALO), SPAN)])
        return carry

    pick(0, ends[0])
    pick(windows - 1, ends[1])
    lax.fori_loop(1, windows - 1, pick_inner, 0)
    fetch[0].wait()
    query[...] = mm(normed[...], w_q[...]).astype(BF16)
    for copy in fetch[1:]:
        copy.wait()
    keys[...] = mm(gathered[...], w_kv[0]).astype(BF16)
    leave = [
        pltpu.make_async_copy(
            w_parent.at[:, c * features : (c + 1) * features], wp.at[c * features : (c + 1) * features], sems.at[3 + c]
        )
        for c in range(2)
    ]
    for copy in leave:
        copy.start()
    split = early.shape[0]
    tiles = range(features // LANES)

    def scores(w, tile):
        here = slice(w * WIN, (w + 1) * WIN)
        return self_scores(keys[here], query[here], tile, head_size)

    def project_values(begin, end):
        values = mm(gathered[...], w_kv[1][:, begin:end]).astype(BF16)
        for w in range(windows):
            values_t[w, begin:end] = values[w * WIN : (w + 1) * WIN].T

    def apply(w, tile, weights):
        out = early.at[w] if w < split else late.at[w - split]
        for k, weight in enumerate(weights):
            head = slice(tile * LANES + k * head_size, tile * LANES + (k + 1) * head_size)
            out[head] = mm(values_t[w, head], weight).astype(BF16)
        if tile == tiles[-1] and w < split:
            leave.append(pltpu.make_async_copy(out, early_h.at[w], sems.at[5 + w]))
            leave[-1].start()

    pending = [scores(0, tile) for tile in tiles]
    before = []
    for w in range(windows):
        coming, weights = [], []
        for tile in tiles:
            if w + 1 < windows:
                coming.append(scores(w + 1, tile))
            weights.append(self_weights(pending[tile], head_size))
            if w == 0 and tile % 2 == 0:
                project_values(tile * LANES, min(tile + 2, len(tiles)) * LANES)
            if w > 0:
                apply(w - 1, tile, before[tile])
        pending, before = coming, weights
    for tile in tiles:
        apply(windows - 1, tile, before[tile])
    for copy in leave:
        copy.wait()


def cross_kernel(
    query, late, gains, arrived, wp, early_h, fine_h, w_out, out, early, fine, wo, out_s, p_keys, p_values, sems,
    *, windows, head_size, all_rows, tight,
):
    rows, features = fine.shape
    fetch = [
        pltpu.make_async_copy(early_h, early, sems.at[1]),
        pltpu.make_async_copy(w_out, wo, sems.at[2]),
        pltpu.make_async_copy(fine_h, fine, sems.at[3]),
    ]
    for copy in fetch:
        copy.start()
    count = p_keys.shape[0]
    if tight:
        parents, slots = unpack_rows(arrived, count, features)
        place = lax.broadcasted_iota(jnp.int32, (count, count), 0)
        places = jnp.where(place == jnp.broadcast_to(slots, (count, count)), 1.0, 0.0).astype(BF16)
        normed_parents = mm(places, rms_rows(parents, gains[1])).astype(BF16)
    else:
        places = one_hot(arrived[:, features:].astype(F32).astype(jnp.int32), count)
        ordered = mm(places, arrived[:, :features], TN).astype(BF16)
        normed_parents = rms_rows(ordered, gains[1])
    p_keys[...] = mm(normed_parents, wp[:features]).astype(BF16)
    p_values[...] = mm(normed_parents, wp[features:]).astype(BF16)
    split = early.shape[0]
    rows_of = [slice(w * WIN, (w + 1) * WIN) for w in range(windows)]

    def crossed(w):
        own = slice(w * PWIN, (w + 1) * PWIN)
        return cross_attention(p_keys[own], p_values[own], query[rows_of[w]], head_size)

    ahead = [crossed(w) for w in range(2)]
    for copy in fetch:
        copy.wait()
    for w, here in enumerate(rows_of):
        self_t = early[w] if w < split else late[w - split]
        joined = jnp.concatenate([self_t, ahead.pop(0)], axis=0).T
        branch = mm(joined, wo[...])
        out_s[here] = (fine[here].astype(F32) + branch).astype(BF16)
        pltpu.make_async_copy(out_s.at[here], out.at[here], sems.at[0]).start()
        if w + 2 < windows:
            ahead.append(crossed(w + 2))
    pltpu.make_async_copy(out_s, out, sems.at[0]).wait()


def on_device(
    fine_tokens, parent_tokens, shift_table, parent_slot, fine_gain, parent_gain, w_qkv, w_parent, w_out,
):
    rows, features = fine_tokens.shape
    parents = parent_tokens.shape[0]
    devices = lax.axis_size("pix")
    windows = rows // WIN
    share = parents // devices
    tight = share % 16 == 0 and LANES % share == 0 and features % LANES == 0
    packing = (devices, share * (features // LANES) + 16, LANES) if tight else (parents, features + LANES)
    order = tuple((d + devices // 4) % devices for d in range(devices)) if tight else None
    sizes = dict(windows=windows, head_size=features // HEADS, all_rows=rows * devices)
    params = pltpu.CompilerParams(vmem_limit_bytes=32 * MIB)
    semaphores = pltpu.SemaphoreType.DMA

    def near(*shape, dtype=BF16):
        return pltpu.VMEM(shape, dtype)

    def far(x):
        return pltpu.with_memory_space_constraint(x, pltpu.HBM)

    fine, weights = far(fine_tokens), far(w_qkv)
    first, second, packed, fine_v, index, gains = pl.pallas_call(
        functools.partial(pack_kernel, order=order),
        out_shape=[
            near(HALO, features),
            near(HALO, features),
            near(*packing),
            near(rows, features),
            near(windows, 1, WIN, dtype=jnp.int32),
            near(2, 1, features, dtype=F32),
        ],
        in_specs=[HBM] * 6,
        out_specs=[VMEM] * 6,
        scratch_shapes=[
            near(parents, features),
            near(1, parents, dtype=jnp.int32),
            semaphores((8,)),
        ],
        compiler_params=params,
        name="pack",
    )(
        fine, far(parent_tokens), far(parent_slot.reshape(1, parents)), far(shift_table.reshape(windows, 1, WIN)),
        far(fine_gain.reshape(1, features)), far(parent_gain.reshape(1, features)),
    )
    pairs = [(i, i + 1 - 2 * (i % 2)) for i in range(devices)]
    across = [(i, (i - 1 + 2 * (i % 2)) % devices) for i in range(devices)]
    first_in = lax.ppermute(first, "pix", pairs)
    second_in = lax.ppermute(second, "pix", across)
    packed, normed = pl.pallas_call(
        norm_kernel,
        out_shape=[pltpu.HBM(packing, BF16), near(rows, features)],
        in_specs=[VMEM] * 4,
        out_specs=[HBM, VMEM],
        input_output_aliases={2: 1},
        scratch_shapes=[semaphores],
        compiler_params=params,
        name="norm",
    )(second, packed, fine_v, gains)
    groups = [list(order)] if tight else None
    arrived = lax.all_to_all(packed, "pix", split_axis=0, concat_axis=0, tiled=True, axis_index_groups=groups)

    split = windows // 2
    query, early, late, wp = pl.pallas_call(
        functools.partial(self_kernel, **sizes),
        out_shape=[
            near(rows, features),
            pltpu.HBM((split, features, WIN), BF16),
            near(windows - split, features, WIN),
            near(2 * features, features),
        ],
        in_specs=[VMEM] * 5 + [HBM] * 2,
        out_specs=[VMEM, HBM, VMEM, VMEM],
        input_output_aliases={0: 3} if rows == 2 * features else {},
        scratch_shapes=[
            near(features, features),
            near(2, features, features),
            near(split, features, WIN),
            near(2, SPAN, features),
            near(rows, features),
            near(rows, features),
            near(windows, features, WIN),
            semaphores((5 + split,)),
        ],
        compiler_params=params,
        cost_estimate=pl.CostEstimate(flops=16 * 10**9, bytes_accessed=4 * 10**6, transcendentals=4 * 10**6),
        name="self",
    )(normed, index, gains, first_in, second_in, weights, far(w_parent))

    return pl.pallas_call(
        functools.partial(cross_kernel, tight=tight, **sizes),
        out_shape=pltpu.HBM((rows, features), BF16),
        in_specs=[VMEM] * 5 + [HBM] * 3,
        out_specs=HBM,
        scratch_shapes=[
            near(split, features, WIN),
            near(rows, features),
            near(2 * features, features),
            near(rows, features),
            near(parents, features),
            near(parents, features),
            semaphores((4,)),
        ],
        compiler_params=params,
        cost_estimate=pl.CostEstimate(flops=5 * 10**9, bytes_accessed=6 * 10**6, transcendentals=10**6),
        name="cross",
    )(query, late, gains, arrived, wp, far(early), fine, far(w_out))


def solution(mesh):
    return jax.shard_map(
        on_device,
        mesh=mesh,
        in_specs=(P(("batch", "pix"), None), P(("batch", "pix"), None), P("pix"), P("pix"), P(), P(), P(), P(), P()),
        out_specs=P(("batch", "pix"), None),
        check_vma=False,
    )
```

```python
import functools
import math

import jax
import jax.numpy as jnp
from jax import lax
from jax.experimental import pallas as pl
from jax.experimental.pallas import tpu as pltpu
from jax.sharding import PartitionSpec as P

HEADS = 16
WIN = 256
HALO = 128
PWIN = 64
LANES = 128
SPAN = WIN + 2 * HALO
F32 = jnp.float32
BF16 = jnp.bfloat16
VMEM = pl.BlockSpec(memory_space=pltpu.VMEM)
HBM = pl.BlockSpec(memory_space=pltpu.HBM)
MIB = 1024 * 1024
NN, NT, TN = ((1,), (0,)), ((1,), (1,)), ((0,), (0,))


def mm(a, b, dims=NN):
    return lax.dot_general(a, b, (dims, ((), ())), preferred_element_type=F32)


def rms_rows(matrix, gain):
    values = matrix.astype(F32)
    factor = lax.rsqrt(jnp.mean(values * values, axis=-1, keepdims=True) + 1e-06)
    return (values * factor * gain).astype(BF16)


def softmax_down(scores, scale):
    powers = jnp.exp2((scores - jnp.max(scores, axis=0, keepdims=True)) * scale)
    return (powers * (1.0 / jnp.sum(powers, axis=0, keepdims=True))).astype(BF16)


def column_of(row):
    wide = jnp.broadcast_to(row, (LANES, row.shape[1]))
    return jnp.concatenate([wide[:, k : k + LANES].T for k in range(0, row.shape[1], LANES)], axis=0)


def one_hot(column, width):
    lane = lax.broadcasted_iota(jnp.int32, column.shape, 1)
    return jnp.concatenate(
        [jnp.where(column == lane + k, 1.0, 0.0).astype(BF16) for k in range(0, width, LANES)], axis=1
    )


def spread(rows, head_size):
    lane = lax.broadcasted_iota(jnp.int32, rows.shape, 1) // head_size
    return jnp.concatenate([jnp.where(lane == k, rows, 0) for k in range(LANES // head_size)], axis=0)


def gather(span, row, first_row, all_rows):
    offset = row - first_row
    offset = jnp.where(offset < 0, offset + all_rows, offset)
    offset = jnp.where(offset >= all_rows, offset - all_rows, offset)
    return mm(one_hot(column_of(offset), SPAN), span).astype(BF16)


def self_scores(keys, query, tile, head_size):
    lanes = slice(tile * LANES, (tile + 1) * LANES)
    return mm(spread(keys[:, lanes], head_size), query[:, lanes], NT)


def self_weights(scores, head_size):
    scale = math.log2(math.e) / math.sqrt(head_size)
    heads = LANES // head_size
    count = scores.shape[0] // heads
    return [softmax_down(scores[k * count : (k + 1) * count], scale) for k in range(heads)]


def cross_attention(keys, values, query, head_size):
    scale = math.log2(math.e) / math.sqrt(head_size)
    per_tile = LANES // head_size
    tiles = [slice(k, k + LANES) for k in range(0, query.shape[1], LANES)]
    scores = [mm(spread(keys[:, tile], head_size), query[:, tile], NT) for tile in tiles]
    out = []
    for tile, score in zip(tiles, scores):
        weights = [softmax_down(score[k * PWIN : (k + 1) * PWIN], scale) for k in range(per_tile)]
        out.append(mm(spread(values[:, tile], head_size), jnp.concatenate(weights, axis=0), TN).astype(BF16))
    return jnp.concatenate(out, axis=0)


def span_start(w, rows):
    return lax.axis_index("pix") * rows + w * WIN - HALO


def block(w, size):
    return pl.ds(pl.multiple_of(w * size, size), size)


def pack_rows(parents, slots, packed, order):
    chunks, height, _ = packed.shape
    count = parents.shape[0] // chunks
    wide = jnp.broadcast_to(slots, (height - count * (parents.shape[1] // LANES), slots.shape[1])).astype(F32)
    for d, owner in enumerate(order):
        own = slice(owner * count, (owner + 1) * count)
        for c in range(parents.shape[1] // LANES):
            packed[d, c * count : (c + 1) * count] = parents[own, c * LANES : (c + 1) * LANES]
        shift = (-owner * count) % slots.shape[1]
        turned = pltpu.roll(wide, shift, 1) if shift else wide
        packed[d, height - wide.shape[0] :] = turned[:, :LANES].astype(BF16)


def unpack_rows(arrived, parents, features):
    chunks, height, _ = arrived.shape
    count = parents // chunks
    tiles = features // LANES
    rows = jnp.concatenate(
        [
            jnp.concatenate([arrived[d, c * count : (c + 1) * count] for d in range(chunks)], axis=0)
            for c in range(tiles)
        ],
        axis=1,
    )
    slots = []
    for d in range(chunks):
        begin = d * count % LANES
        part = arrived[d, tiles * count :].astype(F32)
        if begin == 0:
            slots.append(part)
        else:
            lane = lax.broadcasted_iota(jnp.int32, part.shape, 1)
            slots[-1] = jnp.where(lane < begin, slots[-1], pltpu.roll(part, begin, 1))
    return rows, jnp.concatenate(slots, axis=1)[:1].astype(jnp.int32)


def pack_kernel(
    fine, parents, slots, index, gain, parent_gain, first, second, packed, fine_v, index_v, gains, parents_s, slots_s, sems,
    *, order,
):
    rows, features = fine.shape
    odd = lax.rem(lax.axis_index("pix"), 2)
    pieces = [
        (slots, slots_s),
        (parents, parents_s),
        (fine.at[pl.ds(pl.multiple_of((1 - odd) * (rows - HALO), HALO), HALO)], first),
        (fine.at[pl.ds(pl.multiple_of(odd * (rows - HALO), HALO), HALO)], second),
        (gain, gains.at[0]),
        (parent_gain, gains.at[1]),
        (index, index_v),
    ]
    pieces += [(fine.at[k : k + WIN], fine_v.at[k : k + WIN]) for k in range(0, rows, WIN)]
    copies = [pltpu.make_async_copy(src, dst, sems.at[k]) for k, (src, dst) in enumerate(pieces)]
    for copy in copies:
        copy.start()
    copies[0].wait()
    copies[1].wait()
    if order:
        pack_rows(parents_s, slots_s[...], packed, order)
    else:
        packed[:, :features] = parents_s[...]
        packed[:, features:] = column_of(slots_s[...]).astype(F32).astype(BF16)
    for copy in copies[2:]:
        copy.wait()


def norm_kernel(before, packed, fine, gains, passed, normed, sem):
    copy = pltpu.make_async_copy(packed, passed, sem)
    copy.start()
    for start in range(0, fine.shape[0], WIN):
        normed[start : start + WIN] = rms_rows(fine[start : start + WIN], gains[0])
    copy.wait()


def self_kernel(
    normed, index, gains, first, second, w_qkv, w_parent, query, early_h, late, wp, w_q, w_kv, early, ends, gathered, keys,
    values_t, sems,
    *, windows, head_size, all_rows,
):
    rows, features = normed.shape
    own = SPAN - HALO
    fetch = [
        pltpu.make_async_copy(w_qkv.at[:, c * features : (c + 1) * features], to, sems.at[c])
        for c, to in enumerate([w_q, w_kv.at[0], w_kv.at[1]])
    ]
    for copy in fetch:
        copy.start()
    odd = lax.rem(lax.axis_index("pix"), 2) == 1
    ends[0, :HALO] = rms_rows(jnp.where(odd, first[...], second[...]), gains[0])
    ends[0, HALO:] = normed[:own]
    ends[1, :own] = normed[rows - own :]
    ends[1, own:] = rms_rows(jnp.where(odd, second[...], first[...]), gains[0])

    def pick(w, span):
        gathered[block(w, WIN)] = gather(span, index[w], span_start(w, rows), all_rows)

    def pick_inner(w, carry):
        pick(w, normed[pl.ds(pl.multiple_of(w * WIN - HALO, HALO), SPAN)])
        return carry

    pick(0, ends[0])
    pick(windows - 1, ends[1])
    lax.fori_loop(1, windows - 1, pick_inner, 0)
    fetch[0].wait()
    query[...] = mm(normed[...], w_q[...]).astype(BF16)
    for copy in fetch[1:]:
        copy.wait()
    keys[...] = mm(gathered[...], w_kv[0]).astype(BF16)
    leave = [
        pltpu.make_async_copy(
            w_parent.at[:, c * features : (c + 1) * features], wp.at[c * features : (c + 1) * features], sems.at[3 + c]
        )
        for c in range(2)
    ]
    for copy in leave:
        copy.start()
    split = early.shape[0]
    tiles = range(features // LANES)

    def scores(w, tile):
        here = slice(w * WIN, (w + 1) * WIN)
        return self_scores(keys[here], query[here], tile, head_size)

    def project_values(begin, end):
        values = mm(gathered[...], w_kv[1][:, begin:end]).astype(BF16)
        for w in range(windows):
            values_t[w, begin:end] = values[w * WIN : (w + 1) * WIN].T

    def apply(w, tile, weights):
        out = early.at[w] if w < split else late.at[w - split]
        for k, weight in enumerate(weights):
            head = slice(tile * LANES + k * head_size, tile * LANES + (k + 1) * head_size)
            out[head] = mm(values_t[w, head], weight).astype(BF16)
        if tile == tiles[-1] and w < split:
            leave.append(pltpu.make_async_copy(out, early_h.at[w], sems.at[5 + w]))
            leave[-1].start()

    pending = [scores(0, tile) for tile in tiles]
    before = []
    for w in range(windows):
        coming, weights = [], []
        for tile in tiles:
            if w + 1 < windows:
                coming.append(scores(w + 1, tile))
            weights.append(self_weights(pending[tile], head_size))
            if w == 0 and tile % 2 == 0:
                project_values(tile * LANES, min(tile + 2, len(tiles)) * LANES)
            if w > 0:
                apply(w - 1, tile, before[tile])
        pending, before = coming, weights
    for tile in tiles:
        apply(windows - 1, tile, before[tile])
    for copy in leave:
        copy.wait()


def cross_kernel(
    query, late, gains, arrived, wp, early_h, fine_h, w_out, out, early, fine, wo, out_s, p_keys, p_values, sems,
    *, windows, head_size, all_rows, tight,
):
    rows, features = fine.shape
    fetch = [
        pltpu.make_async_copy(early_h, early, sems.at[1]),
        pltpu.make_async_copy(w_out, wo, sems.at[2]),
        pltpu.make_async_copy(fine_h, fine, sems.at[3]),
    ]
    for copy in fetch:
        copy.start()
    count = p_keys.shape[0]
    if tight:
        parents, slots = unpack_rows(arrived, count, features)
        place = lax.broadcasted_iota(jnp.int32, (count, count), 0)
        places = jnp.where(place == jnp.broadcast_to(slots, (count, count)), 1.0, 0.0).astype(BF16)
        ordered = mm(places, parents).astype(BF16)
    else:
        places = one_hot(arrived[:, features:].astype(F32).astype(jnp.int32), count)
        ordered = mm(places, arrived[:, :features], TN).astype(BF16)
    normed_parents = rms_rows(ordered, gains[1])
    p_keys[...] = mm(normed_parents, wp[:features]).astype(BF16)
    p_values[...] = mm(normed_parents, wp[features:]).astype(BF16)
    split = early.shape[0]
    rows_of = [slice(w * WIN, (w + 1) * WIN) for w in range(windows)]

    def crossed(w):
        own = slice(w * PWIN, (w + 1) * PWIN)
        return cross_attention(p_keys[own], p_values[own], query[rows_of[w]], head_size)

    ahead = [crossed(w) for w in range(2)]
    for copy in fetch:
        copy.wait()
    for w, here in enumerate(rows_of):
        self_t = early[w] if w < split else late[w - split]
        joined = jnp.concatenate([self_t, ahead.pop(0)], axis=0).T
        branch = mm(joined, wo[...])
        out_s[here] = (fine[here].astype(F32) + branch).astype(BF16)
        pltpu.make_async_copy(out_s.at[here], out.at[here], sems.at[0]).start()
        if w + 2 < windows:
            ahead.append(crossed(w + 2))
    pltpu.make_async_copy(out_s, out, sems.at[0]).wait()


def on_device(
    fine_tokens, parent_tokens, shift_table, parent_slot, fine_gain, parent_gain, w_qkv, w_parent, w_out,
):
    rows, features = fine_tokens.shape
    parents = parent_tokens.shape[0]
    devices = lax.axis_size("pix")
    windows = rows // WIN
    share = parents // devices
    tight = share % 16 == 0 and LANES % share == 0 and features % LANES == 0
    packing = (devices, share * (features // LANES) + 16, LANES) if tight else (parents, features + LANES)
    order = tuple((d + devices // 4) % devices for d in range(devices)) if tight else None
    sizes = dict(windows=windows, head_size=features // HEADS, all_rows=rows * devices)
    params = pltpu.CompilerParams(vmem_limit_bytes=32 * MIB)
    semaphores = pltpu.SemaphoreType.DMA

    def near(*shape, dtype=BF16):
        return pltpu.VMEM(shape, dtype)

    def far(x):
        return pltpu.with_memory_space_constraint(x, pltpu.HBM)

    fine, weights = far(fine_tokens), far(w_qkv)
    first, second, packed, fine_v, index, gains = pl.pallas_call(
        functools.partial(pack_kernel, order=order),
        out_shape=[
            near(HALO, features),
            near(HALO, features),
            near(*packing),
            near(rows, features),
            near(windows, 1, WIN, dtype=jnp.int32),
            near(2, 1, features, dtype=F32),
        ],
        in_specs=[HBM] * 6,
        out_specs=[VMEM] * 6,
        scratch_shapes=[
            near(parents, features),
            near(1, parents, dtype=jnp.int32),
            semaphores((7 + windows,)),
        ],
        compiler_params=params,
        name="pack",
    )(
        fine, far(parent_tokens), far(parent_slot.reshape(1, parents)), far(shift_table.reshape(windows, 1, WIN)),
        far(fine_gain.reshape(1, features)), far(parent_gain.reshape(1, features)),
    )
    pairs = [(i, i + 1 - 2 * (i % 2)) for i in range(devices)]
    across = [(i, (i - 1 + 2 * (i % 2)) % devices) for i in range(devices)]
    first_in = lax.ppermute(first, "pix", pairs)
    second_in = lax.ppermute(second, "pix", across)
    packed, normed = pl.pallas_call(
        norm_kernel,
        out_shape=[pltpu.HBM(packing, BF16), near(rows, features)],
        in_specs=[VMEM] * 4,
        out_specs=[HBM, VMEM],
        input_output_aliases={2: 1},
        scratch_shapes=[semaphores],
        compiler_params=params,
        name="norm",
    )(second, packed, fine_v, gains)
    groups = [list(order)] if tight else None
    arrived = lax.all_to_all(packed, "pix", split_axis=0, concat_axis=0, tiled=True, axis_index_groups=groups)

    split = windows // 2
    query, early, late, wp = pl.pallas_call(
        functools.partial(self_kernel, **sizes),
        out_shape=[
            near(rows, features),
            pltpu.HBM((split, features, WIN), BF16),
            near(windows - split, features, WIN),
            near(2 * features, features),
        ],
        in_specs=[VMEM] * 5 + [HBM] * 2,
        out_specs=[VMEM, HBM, VMEM, VMEM],
        input_output_aliases={0: 3} if rows == 2 * features else {},
        scratch_shapes=[
            near(features, features),
            near(2, features, features),
            near(split, features, WIN),
            near(2, SPAN, features),
            near(rows, features),
            near(rows, features),
            near(windows, features, WIN),
            semaphores((5 + split,)),
        ],
        compiler_params=params,
        cost_estimate=pl.CostEstimate(flops=16 * 10**9, bytes_accessed=4 * 10**6, transcendentals=4 * 10**6),
        name="self",
    )(normed, index, gains, first_in, second_in, weights, far(w_parent))

    return pl.pallas_call(
        functools.partial(cross_kernel, tight=tight, **sizes),
        out_shape=pltpu.HBM((rows, features), BF16),
        in_specs=[VMEM] * 5 + [HBM] * 3,
        out_specs=HBM,
        scratch_shapes=[
            near(split, features, WIN),
            near(rows, features),
            near(2 * features, features),
            near(rows, features),
            near(parents, features),
            near(parents, features),
            semaphores((4,)),
        ],
        compiler_params=params,
        cost_estimate=pl.CostEstimate(flops=5 * 10**9, bytes_accessed=6 * 10**6, transcendentals=10**6),
        name="cross",
    )(query, late, gains, arrived, wp, far(early), fine, far(w_out))


def solution(mesh):
    return jax.shard_map(
        on_device,
        mesh=mesh,
        in_specs=(P(("batch", "pix"), None), P(("batch", "pix"), None), P("pix"), P("pix"), P(), P(), P(), P(), P()),
        out_specs=P(("batch", "pix"), None),
        check_vma=False,
    )
```
